128 devices in a mesh: view: 4 (over x), blk: 32 (over z, y, core).
Axes of the slice: x: 4, y: 4, z: 4, core: 2. Of those that a mesh axis runs over, the one named last changes fastest.
Arguments:
- estimate: float32 [1024, 128, 512], P('blk'), may hold values from 0.15 to 6.7
- views: float32 [4, 1024, 128, 512], P('view', 'blk'), may hold values from 0.15 to 6.7
- psf: float32 [4, 3, 33], P('view'), may hold values from 0.05 to 1
- offsets: int32 [4, 3], P('view'), may hold values from 0 to 16, as said below
Outputs:
- updated: float32 [1024, 128, 512], P('blk')
The draws below stay inside these ranges and needn't reach their ends.
Inputs may be any that keep to these rules, and one draw needn't show every extreme that they name: Voxel p of a view's grid lies at voxel p + offsets of the estimate's grid along each dimension.
All inputs are finite; a program needn't handle non-finite values.
Results may differ from the reference program's by a relative error of at most 0.00007.
Values sent between devices are 32-bit elements; how exact they have to be, the bound alone decides.
No kernel may reach another device: no remote copies, remote signals or barrier semaphores. Data moves between devices by JAX's collectives and lax.ppermute only.
A program may use at most 192 MiB of HBM per device.

```python
import math
import jax
import jax.numpy as jnp
from jax import lax

NY = 128
NZ = 512
RADIUS = 16
KERN = 33
VIEWS = 4
NX = 1024


def plane_waves(key, leading, amplitude):
    sub_keys = jax.random.split(key, 3)
    periods = jax.random.randint(sub_keys[0], (leading, 3, 3), 32, 129).astype(jnp.int32)
    flip_sign = jax.random.randint(sub_keys[1], (leading, 3, 3), 0, 2).astype(jnp.int32)
    phases = jax.random.uniform(sub_keys[2], (leading, 3), jnp.float32, 0.0, 2.0 * math.pi)
    coords = [jnp.arange(NX, dtype=jnp.int32), jnp.arange(NY, dtype=jnp.int32), jnp.arange(NZ, dtype=jnp.int32)]
    lengths = [NX, NY, NZ]
    summed = jnp.zeros((leading, NX, NY, NZ), jnp.float32)
    for wave_index in range(3):
        angles = phases[:, wave_index].reshape(leading, 1, 1, 1)
        for dim_index in range(3):
            period = periods[:, wave_index, dim_index][:, None]
            residue = coords[dim_index][None, :] % period
            residue = jnp.where(flip_sign[:, wave_index, dim_index][:, None] == 1, period - residue, residue)
            lag_term = 2.0 * math.pi * residue.astype(jnp.float32) / period.astype(jnp.float32)
            target = [leading, 1, 1, 1]
            target[dim_index + 1] = lengths[dim_index]
            angles = angles + lag_term.reshape(target)
        summed = summed + amplitude * jnp.cos(angles)
    return summed


def draw_estimate(key, part):
    key = jax.random.fold_in(key, 11)
    wave_key, rough_key = jax.random.split(key)
    field = plane_waves(wave_key, 1, 0.4)
    rough = jnp.exp(jax.random.uniform(rough_key, (1, NX, NY, NZ), jnp.float32, math.log(0.5), math.log(2.0)))
    return (rough * jnp.exp(field))[0].astype(jnp.float32)


def draw_views(key, part):
    key = jax.random.fold_in(key, 13)
    wave_key, rough_key = jax.random.split(key)
    field = plane_waves(wave_key, VIEWS, 0.4)
    rough = jnp.exp(jax.random.uniform(rough_key, (VIEWS, NX, NY, NZ), jnp.float32, math.log(0.5), math.log(2.0)))
    return (rough * jnp.exp(field)).astype(jnp.float32)


def draw_offsets(key, part):
    key = jax.random.fold_in(key, 7)
    first_key, second_key = jax.random.split(key)
    values = jax.random.randint(first_key, (VIEWS, 3), 0, RADIUS + 1).astype(jnp.int32)
    chosen = jax.random.randint(second_key, (), 0, VIEWS).astype(jnp.int32)
    values = values.at[chosen, 0].set(RADIUS)
    values = values.at[(chosen + 1) % VIEWS, 0].set(0)
    return values


def level_of(own_key, dims, shards, low, high):
    level, own = 1.0, jax.random.fold_in(own_key, 6)
    for position, shards_of in shards:
        steps = jnp.exp(jax.random.uniform(jax.random.fold_in(own, position), (shards_of,), jnp.float32, low / len(shards), high / len(shards)))
        level = level * jnp.repeat(steps, dims[position] // shards_of).reshape([-1 if axis == position else 1 for axis in range(len(dims))])
    return level


def setup_inputs(seed: int = 0) -> dict:
    keys = jax.random.split(jax.random.key(seed), 5)
    return {
        "estimate": draw_estimate(jax.random.fold_in(keys[4], 71), 0),
        "views": draw_views(jax.random.fold_in(keys[4], 71), 0),
        "psf": jnp.clip(jnp.exp(math.log(1.0) - 2.9957323 * jax.random.uniform(keys[2], (VIEWS, 3, KERN), jnp.float32) ** level_of(keys[2], (VIEWS, 3, KERN), ((0, 4),), -0.2, 0.2)), 0.05, 1.0),
        "offsets": draw_offsets(jax.random.fold_in(keys[4], 71), 0),
    }


background = 0.1


def blur_along(volume, taps, shift_by, axis_dim):
    count = volume.shape[axis_dim]
    widths = [(0, 0), (0, 0), (0, 0)]
    widths[axis_dim] = (RADIUS, 2 * RADIUS)
    padded = jnp.pad(volume, widths)
    result = jnp.zeros_like(volume)
    for lag_step in range(KERN):
        start = (shift_by + 2 * RADIUS - lag_step).astype(jnp.int32)
        result = result + taps[lag_step] * lax.dynamic_slice_in_dim(padded, start, count, axis_dim)
    return result


def unblur_along(volume, taps, shift_by, axis_dim):
    count = volume.shape[axis_dim]
    widths = [(0, 0), (0, 0), (0, 0)]
    widths[axis_dim] = (2 * RADIUS, RADIUS)
    padded = jnp.pad(volume, widths)
    result = jnp.zeros_like(volume)
    for lag_step in range(KERN):
        start = (lag_step - shift_by + RADIUS).astype(jnp.int32)
        result = result + taps[lag_step] * lax.dynamic_slice_in_dim(padded, start, count, axis_dim)
    return result


def reference(estimate, views, psf, offsets):
    kernel = psf / jnp.sum(psf, axis=2, keepdims=True)
    correction = jnp.zeros(estimate.shape, jnp.float32)
    for view_index in range(VIEWS):
        forward = estimate
        for dim_index in range(3):
            forward = blur_along(forward, kernel[view_index, dim_index], offsets[view_index, dim_index], dim_index)
        ratios = views[view_index] / (forward + background)
        spread = ratios
        for dim_index in range(3):
            spread = unblur_along(spread, kernel[view_index, dim_index], offsets[view_index, dim_index], dim_index)
        correction = correction + spread
    return estimate * correction / VIEWS
```

```python
import jax
import jax.numpy as jnp
from jax import lax
from jax.experimental import pallas as pl
from jax.experimental.pallas import tpu as pltpu
from jax.sharding import PartitionSpec as P

RADIUS = 16
KERN = 33
LEFT = RADIUS
RIGHT = 2 * RADIUS
QUARTER = 128
WIDE = LEFT + QUARTER + RIGHT
SLAB = 32
TALL = LEFT + SLAB + RIGHT
VIEWS = 4
BACKGROUND = 0.1
VMEM = 48 * 1024 * 1024

f32 = jnp.float32
bf16 = jnp.bfloat16


def call(kernel, out_shape, grid, in_specs, out_specs, prefetch=0, aliases=None, flops=0, moved=0):
    return pl.pallas_call(
        kernel,
        out_shape=out_shape,
        grid_spec=pltpu.PrefetchScalarGridSpec(
            num_scalar_prefetch=prefetch, grid=grid, in_specs=in_specs, out_specs=out_specs
        ),
        input_output_aliases=aliases or {},
        compiler_params=pltpu.CompilerParams(vmem_limit_bytes=VMEM),
        cost_estimate=pl.CostEstimate(flops=flops, bytes_accessed=moved, transcendentals=0),
    )


def shape(*dims, dtype=f32):
    return jax.ShapeDtypeStruct(dims, dtype)


def halves(x):
    high = x.astype(bf16)
    low = (x - high.astype(f32)).astype(bf16)
    return high, low


def stacked(x, axis, blank=0):
    high, low = halves(x)
    parts = [high, low, high]
    if blank:
        dims = list(x.shape)
        dims[axis] = blank
        parts.append(jnp.zeros(dims, bf16))
    return jnp.concatenate(parts, axis=axis)


def dot(a, b):
    return lax.dot_general(a, b, (((1,), (0,)), ((), ())), preferred_element_type=f32)


def dot_nt(a, b):
    return lax.dot_general(a, b, (((1,), (1,)), ((), ())), preferred_element_type=f32)


def lag_taps(params, slot, dim, lag):
    value = jnp.zeros(lag.shape, f32)
    for tap in range(KERN):
        value = jnp.where(lag == tap, params[slot, dim, tap], value)
    return value


def thirds(value, part):
    high = value.astype(bf16).astype(f32)
    return jnp.where(part == 2, value - high, high).astype(bf16)


def grid_of(rows, columns):
    return (
        lax.broadcasted_iota(jnp.int32, (rows, columns), 0),
        lax.broadcasted_iota(jnp.int32, (rows, columns), 1),
    )


def bands_kernel(params, ax, az, ay, ayt, azt, axt):
    def offset(slot, dim):
        return params[slot, dim, KERN].astype(jnp.int32)

    row, lane = grid_of(SLAB, 256)
    part = lane // TALL
    spot = lane - part * TALL
    for slot in range(VIEWS):
        lag = row + offset(slot, 0) - spot + 2 * RADIUS
        lag = jnp.where(part < 3, lag, -1)
        ax[slot * SLAB : (slot + 1) * SLAB, :] = thirds(lag_taps(params, slot, 0, lag), part)
    row, lane = grid_of(QUARTER, 512)
    span = QUARTER + 2 * RADIUS
    part = lane // span
    spot = lane - part * span
    for slot in range(VIEWS):
        lag = jnp.where(part < 3, row - spot + 2 * RADIUS, -1)
        az[slot] = thirds(lag_taps(params, slot, 2, lag), part)
    row, lane = grid_of(128, 384)
    part = lane // 128
    spot = lane - part * 128
    for slot in range(VIEWS):
        lag = row + offset(slot, 1) - spot + RADIUS
        ay[slot] = thirds(lag_taps(params, slot, 1, lag), part)
        lag = spot + offset(slot, 1) - row + RADIUS
        ayt[slot] = thirds(lag_taps(params, slot, 1, lag), part)
    row, lane = grid_of(WIDE, 384)
    part = lane // 128
    spot = lane - part * 128
    for slot in range(VIEWS):
        lag = spot + offset(slot, 2) - row + 2 * RADIUS
        azt[slot] = thirds(lag_taps(params, slot, 2, lag), part)
    row, lane = grid_of(TALL, 384)
    part = lane // 128
    spot = lane - part * 128
    owner = spot // SLAB
    plane = spot - owner * SLAB
    value = jnp.zeros((TALL, 384), f32)
    for slot in range(VIEWS):
        lag = plane + offset(slot, 0) - row + 2 * RADIUS
        value = jnp.where(owner == slot, lag_taps(params, slot, 0, lag), value)
    axt[...] = thirds(value, part)


def bands(params):
    whole = pl.BlockSpec(memory_space=pltpu.VMEM)
    return pl.pallas_call(
        bands_kernel,
        out_shape=(
            shape(VIEWS * SLAB, 256, dtype=bf16),
            shape(VIEWS, QUARTER, 512, dtype=bf16),
            shape(VIEWS, 128, 384, dtype=bf16),
            shape(VIEWS, 128, 384, dtype=bf16),
            shape(VIEWS, WIDE, 384, dtype=bf16),
            shape(TALL, 384, dtype=bf16),
        ),
        in_specs=[pl.BlockSpec(memory_space=pltpu.SMEM)],
        out_specs=(whole,) * 6,
        compiler_params=pltpu.CompilerParams(vmem_limit_bytes=VMEM),
    )(params)


def window_kernel(spot, left, middle, right, out):
    q = spot[0]
    for i in range(middle.shape[0]):
        before = left[i].T[QUARTER - LEFT :, :]
        after = right[i].T[:RIGHT, :]
        out[i, :LEFT, :] = jnp.where(q > 0, before, 0.0)
        out[i, LEFT : LEFT + QUARTER, :] = middle[i].T
        out[i, LEFT + QUARTER :, :] = jnp.where(q < VIEWS - 1, after, 0.0)


def window(estimate, spot):
    n = 4
    block = (n, 128, QUARTER)
    return call(
        window_kernel,
        shape(SLAB, WIDE, 128),
        (SLAB // n,),
        [
            pl.BlockSpec(block, lambda i, s: (i, 0, jnp.maximum(s[0] - 1, 0))),
            pl.BlockSpec(block, lambda i, s: (i, 0, s[0])),
            pl.BlockSpec(block, lambda i, s: (i, 0, jnp.minimum(s[0] + 1, VIEWS - 1))),
        ],
        pl.BlockSpec((n, WIDE, 128), lambda i, s: (i, 0, 0)),
        prefetch=1,
        moved=9 << 20,
    )(spot, estimate, estimate, estimate)


def blur_x_kernel(ax, lower, middle, upper, out):
    for z in range(0, middle.shape[1], 2):
        columns = [
            jnp.concatenate([lower[:, c, :], middle[:, c, :], upper[:, c, :]], axis=0)
            for c in (z, z + 1)
        ]
        data = stacked(jnp.concatenate(columns, axis=1), 0, 256 - 3 * TALL)
        result = dot(ax[...], data)
        out[:, z, :] = result[:, :128]
        out[:, z + 1, :] = result[:, 128:]


def blur_x(ax, lower, middle, upper):
    n = 16
    return call(
        blur_x_kernel,
        shape(VIEWS * SLAB, WIDE, 128),
        (WIDE // n,),
        [
            pl.BlockSpec(ax.shape, lambda i: (0, 0)),
            pl.BlockSpec((LEFT, n, 128), lambda i: (0, i, 0)),
            pl.BlockSpec((SLAB, n, 128), lambda i: (0, i, 0)),
            pl.BlockSpec((RIGHT, n, 128), lambda i: (0, i, 0)),
        ],
        pl.BlockSpec((VIEWS * SLAB, n, 128), lambda i: (0, i, 0)),
        flops=6 << 30,
        moved=18 << 20,
    )(ax, lower, middle, upper)


def forward_kernel(starts, az, ay, blurred, out):
    start = starts[pl.program_id(0)]
    span = QUARTER + 2 * RADIUS
    for i in range(0, blurred.shape[0], 2):
        planes = [blurred[j, pl.ds(start, span), :] for j in (i, i + 1)]
        data = stacked(jnp.concatenate(planes, axis=1), 0, 512 - 3 * span)
        section = dot(az[0], data)
        section = jnp.concatenate([section[:, :128], section[:, 128:]], axis=0)
        result = dot_nt(ay[0], stacked(section, 1)) + BACKGROUND
        out[i] = result[:, :QUARTER]
        out[i + 1] = result[:, QUARTER:]


def forward_of(starts, az, ay, blurred):
    n = 4
    steps = SLAB // n
    return call(
        forward_kernel,
        shape(VIEWS * SLAB, 128, QUARTER),
        (VIEWS, steps),
        [
            pl.BlockSpec((1,) + az.shape[1:], lambda v, i, s: (v, 0, 0)),
            pl.BlockSpec((1,) + ay.shape[1:], lambda v, i, s: (v, 0, 0)),
            pl.BlockSpec((n, WIDE, 128), lambda v, i, s: (v * steps + i, 0, 0)),
        ],
        pl.BlockSpec((n, 128, QUARTER), lambda v, i, s: (v * steps + i, 0, 0)),
        prefetch=1,
        flops=20 << 30,
        moved=20 << 20,
    )(starts, az, ay, blurred)


def back_kernel(spot, ayt, azt, forward, measured, out):
    for i in range(0, forward.shape[0], 2):
        ratios = [measured[j] / forward[j] for j in (i, i + 1)]
        section = dot(ayt[0], stacked(jnp.concatenate(ratios, axis=1), 0))
        section = jnp.concatenate([section[:, :QUARTER], section[:, QUARTER:]], axis=0)
        result = dot_nt(azt[0], stacked(section, 1))
        out[i] = result[:, :128]
        out[i + 1] = result[:, 128:]


def back_of(slot, ayt, azt, forward, measured, spot):
    n = 4
    steps = SLAB // n
    return call(
        back_kernel,
        shape(SLAB, WIDE, 128),
        (steps,),
        [
            pl.BlockSpec((1,) + ayt.shape[1:], lambda i, s: (slot, 0, 0)),
            pl.BlockSpec((1,) + azt.shape[1:], lambda i, s: (slot, 0, 0)),
            pl.BlockSpec((n, 128, QUARTER), lambda i, s: (slot * steps + i, 0, 0)),
            pl.BlockSpec((n, 128, QUARTER), lambda i, s: (i, 0, s[0])),
        ],
        pl.BlockSpec((n, WIDE, 128), lambda i, s: (i, 0, 0)),
        prefetch=1,
        flops=5 << 30,
        moved=7 << 20,
    )(spot, ayt, azt, forward, measured)


def spread_x_kernel(axt, a, b, c, d, below, own, above):
    for z in range(0, a.shape[1], 2):
        columns = [
            jnp.concatenate([ref[:, k, :] for ref in (a, b, c, d)], axis=0) for k in (z, z + 1)
        ]
        result = dot(axt[...], stacked(jnp.concatenate(columns, axis=1), 0))
        for k in (0, 1):
            piece = result[:, k * 128 : (k + 1) * 128]
            below[:, z + k, :] = piece[:LEFT]
            own[:, z + k, :] = piece[LEFT : LEFT + SLAB]
            above[:, z + k, :] = piece[LEFT + SLAB :]


def spread_x(axt, spreads):
    n = 16
    sizes = (LEFT, SLAB, RIGHT)
    return call(
        spread_x_kernel,
        tuple(shape(k, WIDE, 128) for k in sizes),
        (WIDE // n,),
        [pl.BlockSpec(axt.shape, lambda i: (0, 0))]
        + [pl.BlockSpec((SLAB, n, 128), lambda i: (0, i, 0))] * VIEWS,
        tuple(pl.BlockSpec((k, n, 128), lambda i: (0, i, 0)) for k in sizes),
        flops=6 << 30,
        moved=18 << 20,
    )(axt, *spreads)


def finish_kernel(spot, estimate, own, lower, upper, near, far, *refs):
    out = refs[-1]
    q = spot[0]
    for i in range(estimate.shape[0]):
        opposite = jnp.concatenate([near[i], far[i]], axis=0)
        for step, piece in ((0, own[i]), (1, lower[i]), (2, opposite), (3, upper[i])):
            where = lax.rem(q + VIEWS - step, VIEWS)
            lanes = pl.ds(pl.multiple_of(where * QUARTER, QUARTER), QUARTER)
            out[i, :, lanes] = estimate[i, :, lanes] * piece.T / VIEWS


def finish(first, spot, estimate, pieces, before):
    n = 4
    planes = pieces[0].shape[0]
    base = first // n
    wide = pl.BlockSpec((n, 128, VIEWS * QUARTER), lambda i, s: (base + i, 0, 0))
    full = pl.BlockSpec((n, QUARTER, 128), lambda i, s: (i, 0, 0))
    half = pl.BlockSpec((n, QUARTER // 2, 128), lambda i, s: (i, 0, 0))
    specs = [wide, full, full, full, half, half]
    arrays = [spot, estimate, *pieces]
    aliases = {}
    if before is not None:
        specs.append(pl.BlockSpec(memory_space=pl.ANY))
        arrays.append(before)
        aliases = {len(arrays) - 1: 0}
    return call(
        finish_kernel,
        shape(*estimate.shape),
        (planes // n,),
        specs,
        wide,
        prefetch=1,
        aliases=aliases,
        moved=planes * 3 << 18,
    )(*arrays)


def along_blk(x, distance):
    size = lax.axis_size("blk")
    route = [(i, i + distance) for i in range(size) if 0 <= i + distance < size]
    return lax.ppermute(x, "blk", route)


def around_view(x, distance):
    return lax.ppermute(x, "view", [(i, (i + distance) % VIEWS) for i in range(VIEWS)])


def along_view(x, distance):
    route = [(i, i + distance) for i in range(VIEWS) if 0 <= i + distance < VIEWS]
    return lax.ppermute(x, "view", route)


def body(estimate, views, psf, offsets):
    q = lax.axis_index("view")
    spot = q[None]
    zero = jnp.zeros((1,), jnp.int32)
    recorded = views[0]
    kernel = psf[0] / jnp.sum(psf[0], axis=1, keepdims=True)
    mine = jnp.concatenate([kernel, offsets[0].astype(f32)[:, None]], axis=1)
    params = jnp.stack([mine] + [around_view(mine, s) for s in (1, 2, 3)])
    starts = params[:, 2, KERN].astype(jnp.int32)

    measured = {0: recorded}
    for s in (1, 3, 2):
        start = lax.rem(q + s, VIEWS) * QUARTER
        measured[s] = around_view(lax.dynamic_slice_in_dim(recorded, start, QUARTER, 2), s)

    middle = window(estimate, spot)
    upper = along_blk(middle, -1)
    lower = along_blk(middle[SLAB - LEFT :], 1)
    ax, az, ay, ayt, azt, axt = bands(params)
    blurred = blur_x(ax, lower, middle, upper)
    forward = forward_of(starts, az, ay, blurred)
    spreads = [None] * VIEWS
    for s in (0, 1, 3, 2):
        spreads[s] = back_of(s, ayt, azt, forward, measured[s], spot if s == 0 else zero)
    below, own, above = spread_x(axt, spreads)

    out = None
    half = SLAB // 2
    for first in (0, half):
        piece = own[first : first + half] + along_blk(above[first : first + half], 1)
        if first:
            piece = piece + along_blk(below, -1)
        from_right = along_view(piece[:, :LEFT], -1)
        from_left = along_view(piece[:, LEFT + QUARTER :], 1)
        piece = piece[:, LEFT : LEFT + QUARTER]
        piece = piece + jnp.pad(from_right, ((0, 0), (QUARTER - LEFT, 0), (0, 0)))
        piece = piece + jnp.pad(from_left, ((0, 0), (0, QUARTER - RIGHT), (0, 0)))
        left = around_view(piece, 1)
        right = around_view(piece, 3)
        near = around_view(left[:, : QUARTER // 2], 1)
        far = around_view(right[:, QUARTER // 2 :], 3)
        out = finish(first, spot, estimate, (piece, left, right, near, far), out)
    return out


def solution(mesh):
    placed = (
        P("blk", None, None),
        P("view", "blk", None, None),
        P("view", None, None),
        P("view", None),
    )
    return jax.shard_map(
        body, mesh=mesh, in_specs=placed, out_specs=P("blk", None, None), check_vma=False
    )
```

```python
import jax
import jax.numpy as jnp
from jax import lax
from jax.experimental import pallas as pl
from jax.experimental.pallas import tpu as pltpu
from jax.sharding import PartitionSpec as P

RADIUS = 16
KERN = 33
LEFT = RADIUS
RIGHT = 2 * RADIUS
QUARTER = 128
WIDE = LEFT + QUARTER + RIGHT
SLAB = 32
TALL = LEFT + SLAB + RIGHT
VIEWS = 4
BACKGROUND = 0.1
ALL = (0, 1, 3, 2)
ROWS = 64
PACKED = ROWS // 2
CHUNK = ROWS + PACKED
CUT = 80
ODD = WIDE + 1
SKEW = CHUNK + 1
FREE = 1 << 10
LONG = 1 << 38
SPANS = ((0, 80), (32, 128))
VMEM = 48 * 1024 * 1024

f32 = jnp.float32
bf16 = jnp.bfloat16


def call(kernel, out_shape, grid, in_specs, out_specs, prefetch=0, aliases=None, flops=0, moved=0):
    return pl.pallas_call(
        kernel,
        out_shape=out_shape,
        grid_spec=pltpu.PrefetchScalarGridSpec(
            num_scalar_prefetch=prefetch, grid=grid, in_specs=in_specs, out_specs=out_specs
        ),
        input_output_aliases=aliases or {},
        compiler_params=pltpu.CompilerParams(vmem_limit_bytes=VMEM),
        cost_estimate=pl.CostEstimate(flops=flops, bytes_accessed=moved, transcendentals=0),
    )


def shape(*dims, dtype=f32):
    return jax.ShapeDtypeStruct(dims, dtype)


def halves(x):
    high = x.astype(bf16)
    low = (x - high.astype(f32)).astype(bf16)
    return high, low


def stacked(x, axis, blank=0):
    high, low = halves(x)
    parts = [high, low, high]
    if blank:
        dims = list(x.shape)
        dims[axis] = blank
        parts.append(jnp.zeros(dims, bf16))
    return jnp.concatenate(parts, axis=axis)


def paired(x, total):
    high, low = halves(x)
    parts = [high, low]
    if total > 2 * x.shape[0]:
        parts.append(jnp.zeros((total - 2 * x.shape[0], x.shape[1]), bf16))
    return jnp.concatenate(parts, axis=0)


def dot(a, b):
    return lax.dot_general(a, b, (((1,), (0,)), ((), ())), preferred_element_type=f32)


def dot_nt(a, b):
    return lax.dot_general(a, b, (((1,), (1,)), ((), ())), preferred_element_type=f32)


def lag_taps(params, slot, dim, lag):
    value = jnp.zeros(lag.shape, f32)
    for tap in range(KERN):
        value = jnp.where(lag == tap, params[slot, dim, tap], value)
    return value


def thirds(value, part):
    high = value.astype(bf16).astype(f32)
    return jnp.where(part == 2, value - high, high).astype(bf16)


def split(value):
    high = value.astype(bf16).astype(f32)
    return high, value - high


def grid_of(rows, columns):
    return (
        lax.broadcasted_iota(jnp.int32, (rows, columns), 0),
        lax.broadcasted_iota(jnp.int32, (rows, columns), 1),
    )


def spread_band(params, offset, slots, band):
    total = band.shape[1]
    count = SLAB * len(slots)
    row, lane = grid_of(TALL, total)
    part = lane // count
    spot = lane - part * count
    owner = spot // SLAB
    plane = spot - owner * SLAB
    value = jnp.zeros((TALL, total), f32)
    for place, slot in enumerate(slots):
        lag = plane + offset(slot, 0) - row + 2 * RADIUS
        value = jnp.where(owner == place, lag_taps(params, slot, 0, lag), value)
    high, low = split(value)
    band[:TALL, :] = jnp.where(part < 2, high, 0.0).astype(bf16)
    band[TALL:, :] = jnp.where(part < 1, low, 0.0).astype(bf16)


def bands_kernel(params, *refs):
    ax, az, ay, ayt, wz, every = refs[-6:]

    def offset(slot, dim):
        return params[slot, dim, KERN].astype(jnp.int32)

    row, lane = grid_of(SLAB, 256)
    part = lane // TALL
    spot = lane - part * TALL
    for slot in range(VIEWS):
        lag = row + offset(slot, 0) - spot + 2 * RADIUS
        lag = jnp.where(part < 3, lag, -1)
        ax[slot * SLAB : (slot + 1) * SLAB, :] = thirds(lag_taps(params, slot, 0, lag), part)
    row, lane = grid_of(128, 128)
    part = lane // 32
    tail = lane - part * 32 + 128
    edge = lane % 64
    edge = jnp.where(edge < RIGHT, QUARTER + edge, edge - RIGHT - LEFT)
    for slot in range(VIEWS):
        high, low = split(lag_taps(params, slot, 2, row - lane + 2 * RADIUS))
        az[slot, :, 0:128] = high.astype(bf16)
        az[slot, :, 128:256] = high.astype(bf16)
        az[slot, :, 256:384] = low.astype(bf16)
        lag = jnp.where(part < 3, row - tail + 2 * RADIUS, -1)
        az[slot, :, 384:512] = thirds(lag_taps(params, slot, 2, lag), part)
        high, low = split(lag_taps(params, slot, 1, row + offset(slot, 1) - lane + RADIUS))
        ay[slot, :, 0:128] = high.astype(bf16)
        ay[slot, :, 128:256] = high.astype(bf16)
        ay[slot, :, 256:384] = low.astype(bf16)
        high, low = split(lag_taps(params, slot, 2, row + offset(slot, 2) - lane + RADIUS))
        wz[slot, :128, 0:128] = high.astype(bf16)
        wz[slot, 128:, 0:128] = high.astype(bf16)
        wz[slot, :128, 128:256] = low.astype(bf16)
        wz[slot, 128:, 128:256] = jnp.zeros((128, 128), bf16)
        lag = row + offset(slot, 2) - edge + RADIUS
        lag = jnp.where(lane % 64 < RIGHT + LEFT, lag, -1)
        high, low = split(lag_taps(params, slot, 2, lag))
        wz[slot, :128, 256:384] = jnp.where(lane < 64, high, low).astype(bf16)
        wz[slot, 128:, 256:384] = jnp.where(lane < 64, high, 0.0).astype(bf16)
    row, lane = grid_of(ROWS, 256)
    for chunk, (first, last) in enumerate(SPANS):
        count = last - first
        part = lane // count
        spot = first + lane - part * count
        for slot in range(VIEWS):
            lag = spot + offset(slot, 1) - (row + chunk * ROWS) + RADIUS
            high, low = split(lag_taps(params, slot, 1, lag))
            ayt[chunk, slot, :ROWS, :] = jnp.where(part < 2, high, 0.0).astype(bf16)
            ayt[chunk, slot, ROWS:, :] = jnp.where(part < 1, low, 0.0).astype(bf16)
    spread_band(params, offset, ALL, every)


def bands(params, after):
    whole = pl.BlockSpec(memory_space=pltpu.VMEM)
    shapes = (
        shape(VIEWS * SLAB, 256, dtype=bf16),
        shape(VIEWS, QUARTER, 512, dtype=bf16),
        shape(VIEWS, 128, 384, dtype=bf16),
        shape(2, VIEWS, 2 * ROWS, 256, dtype=bf16),
        shape(VIEWS, 256, 384, dtype=bf16),
        shape(2 * TALL, 256, dtype=bf16),
    )
    return pl.pallas_call(
        bands_kernel,
        out_shape=shapes,
        in_specs=[pl.BlockSpec(memory_space=pltpu.SMEM)]
        + [pl.BlockSpec(memory_space=pl.ANY)] * len(after),
        out_specs=(whole,) * len(shapes),
        compiler_params=pltpu.CompilerParams(vmem_limit_bytes=VMEM),
        cost_estimate=pl.CostEstimate(flops=FREE, bytes_accessed=FREE, transcendentals=0),
    )(params, *after)


def pack_kernel(psf, offsets, *refs):
    out = refs[-1]
    taps = psf[...]
    out[:, :KERN] = taps / jnp.sum(taps, axis=1, keepdims=True)
    out[:, KERN:] = offsets[...]


def pack(psf, offsets, after):
    return small(pack_kernel, shape(3, KERN + 1), (psf, offsets), after, FREE)


def mark_kernel(*refs):
    refs[-1][...] = jnp.zeros(refs[-1].shape, f32)


def mark(after):
    return small(mark_kernel, shape(8, 128), (), after, LONG)


def window_kernel(spot, left, middle, right, *refs):
    out, low, flat = refs[-3:]
    q = spot[0]
    planes = middle.shape[0]
    for i in range(planes):
        before = left[i].T[QUARTER - LEFT :, :]
        after = right[i].T[:RIGHT, :]
        at = i * ODD
        flat[at : at + LEFT, :] = jnp.where(q > 0, before, 0.0)
        flat[at + LEFT : at + LEFT + QUARTER, :] = middle[i].T
        flat[at + LEFT + QUARTER : at + WIDE, :] = jnp.where(q < VIEWS - 1, after, 0.0)
    for z in range(WIDE):
        row = flat[pl.ds(z, planes, ODD), :]
        out[z] = row
        low[z] = row


def window(estimate, spot, after):
    n = LEFT
    block = (n, 128, QUARTER)
    return pl.pallas_call(
        window_kernel,
        out_shape=(shape(WIDE, SLAB, 128), shape(WIDE, LEFT, 128)),
        grid_spec=pltpu.PrefetchScalarGridSpec(
            num_scalar_prefetch=1,
            grid=(SLAB // n,),
            in_specs=[
                pl.BlockSpec(block, lambda i, s: (i, 0, jnp.maximum(s[0] - 1, 0))),
                pl.BlockSpec(block, lambda i, s: (i, 0, s[0])),
                pl.BlockSpec(block, lambda i, s: (i, 0, jnp.minimum(s[0] + 1, VIEWS - 1))),
            ]
            + [pl.BlockSpec(memory_space=pl.ANY)] * len(after),
            out_specs=(
                pl.BlockSpec((WIDE, n, 128), lambda i, s: (0, i, 0)),
                pl.BlockSpec((WIDE, n, 128), lambda i, s: (0, 0, 0)),
            ),
            scratch_shapes=[pltpu.VMEM((n * ODD + 7, 128), f32)],
        ),
        compiler_params=pltpu.CompilerParams(vmem_limit_bytes=VMEM),
        cost_estimate=pl.CostEstimate(flops=FREE, bytes_accessed=FREE, transcendentals=0),
    )(spot, estimate, estimate, estimate, *after)


def cut_kernel(first, rows, steps, spot, recorded, *refs):
    n = len(steps)
    outs, holds = refs[-2 * n - 2 : -n - 2], refs[-n - 2 : -2]
    sems, out_sems = refs[-2:]
    moves = []
    for k, step in enumerate(steps):
        quarter = lax.rem(spot[0] + step, VIEWS)
        lanes = pl.ds(pl.multiple_of(quarter * QUARTER, QUARTER), QUARTER)
        source = recorded.at[:, pl.ds(first, rows), lanes]
        moves.append(pltpu.make_async_copy(source, holds[k], sems.at[k]))
    for move in moves:
        move.start()
    writes = [pltpu.make_async_copy(holds[k], outs[k], out_sems.at[k]) for k in range(n)]
    for move, write in zip(moves, writes):
        move.wait()
        write.start()
    for write in writes:
        write.wait()


def cut(recorded, spot, first, rows, steps, after=()):
    hbm = pl.BlockSpec(memory_space=pl.ANY)
    return pl.pallas_call(
        lambda *refs: cut_kernel(first, rows, steps, *refs),
        out_shape=(shape(SLAB, rows, QUARTER),) * len(steps),
        in_specs=[pl.BlockSpec(memory_space=pltpu.SMEM)] + [hbm] * (1 + len(after)),
        out_specs=(hbm,) * len(steps),
        scratch_shapes=[pltpu.VMEM((SLAB, rows, QUARTER), f32)] * len(steps)
        + [pltpu.SemaphoreType.DMA((len(steps),))] * 2,
        compiler_params=pltpu.CompilerParams(vmem_limit_bytes=VMEM),
        cost_estimate=pl.CostEstimate(flops=FREE, bytes_accessed=FREE, transcendentals=0),
    )(spot, recorded, *after)


def forward_kernel(starts, ax, az, ay, lower, middle, upper, *refs):
    out, blurred = refs[-2:]
    slot = pl.program_id(0)

    @pl.when(slot == 0)
    def _():
        def some(group, carry):
            at = group * 8
            columns = [
                jnp.concatenate([lower[at + z], middle[at + z], upper[at + z]], axis=0)
                for z in range(8)
            ]
            data = stacked(jnp.concatenate(columns, axis=1), 0, 256 - 3 * TALL)
            result = dot(ax[...], data)
            for z in range(8):
                blurred[pl.ds(at + z, VIEWS * SLAB, ODD), :] = result[:, z * 128 : z * 128 + 128]
            return carry

        lax.fori_loop(0, WIDE // 8, some, 0)

    start = starts[slot]
    span = QUARTER + 2 * RADIUS
    many = 8

    def planes(group, carry):
        first = slot * SLAB + group * many
        data = jnp.concatenate(
            [blurred[pl.ds((first + i) * ODD + start, span), :] for i in range(many)], axis=1
        )
        high, low = halves(data)
        blank = jnp.zeros((32, many * 128), bf16)
        data = [high[:128], low[:128], high[:128], high[128:], low[128:], high[128:], blank]
        section = dot(az[0], jnp.concatenate(data, axis=0))
        section = jnp.concatenate([section[:, i * 128 : i * 128 + 128] for i in range(many)], axis=0)
        result = dot_nt(ay[0], stacked(section, 1)) + BACKGROUND
        for i in range(many):
            out[group * many + i] = result[:, i * QUARTER : (i + 1) * QUARTER]
        return carry

    lax.fori_loop(0, SLAB // many, planes, 0)


def forward_of(starts, ax, az, ay, lower, middle, upper):
    def once(x):
        return pl.BlockSpec(x.shape, lambda v, s: (0,) * x.ndim, pipeline_mode=pl.Buffered(1))

    return pl.pallas_call(
        forward_kernel,
        out_shape=shape(VIEWS * SLAB, 128, QUARTER),
        grid_spec=pltpu.PrefetchScalarGridSpec(
            num_scalar_prefetch=1,
            grid=(VIEWS,),
            in_specs=[
                once(ax),
                pl.BlockSpec((1,) + az.shape[1:], lambda v, s: (v, 0, 0)),
                pl.BlockSpec((1,) + ay.shape[1:], lambda v, s: (v, 0, 0)),
                once(lower),
                once(middle),
                once(upper),
            ],
            out_specs=pl.BlockSpec((SLAB, 128, QUARTER), lambda v, s: (v, 0, 0)),
            scratch_shapes=[pltpu.VMEM((VIEWS * SLAB * ODD + 8, 128), f32)],
        ),
        compiler_params=pltpu.CompilerParams(vmem_limit_bytes=VMEM),
        cost_estimate=pl.CostEstimate(flops=FREE, bytes_accessed=FREE, transcendentals=0),
    )(starts, ax, az, ay, lower, middle, upper)


def adjoint_kernel(chunk, extra, *refs):
    n = VIEWS
    pieces = chunk + 1
    first, last = SPANS[chunk]
    bounds = ((first, CUT), (CUT, 128))[:pieces]
    spot, band, ayt, wz, forward = refs[:5]
    refs = list(refs[5:])
    measured = []
    for slot in ALL:
        if slot == 0:
            lanes = pl.ds(pl.multiple_of(spot[0] * QUARTER, QUARTER), QUARTER)
            whole = refs.pop(0)
            measured.append([whole.at[:, pl.ds(a, b - a), lanes] for a, b in bounds])
        else:
            measured.append([refs.pop(0).at[:, pl.ds(first, CUT - first), :]])
            if chunk:
                measured[-1].append(refs.pop(0))
    refs = refs[extra:]
    outs, refs = refs[:6], refs[6:]
    hold, kept, spread = refs[0], refs[1 : 1 + pieces], refs[1 + pieces]
    totals = refs[2 + pieces : 5 + pieces]
    sems, out_sems = refs[-2:]
    copies = []
    for k, slot in enumerate(ALL):
        source = forward.at[pl.ds(slot * SLAB, SLAB), pl.ds(first, last - first), :]
        moves = [pltpu.make_async_copy(source, hold.at[k], sems.at[k, 0])]
        for piece in range(pieces):
            target = kept[piece].at[k]
            moves.append(pltpu.make_async_copy(measured[k][piece], target, sems.at[k, 1 + piece]))
        for move in moves:
            move.start()
        copies.append(moves)

    many = 8
    lane = lax.broadcasted_iota(jnp.int32, (PACKED, 128), 1)
    for k, slot in enumerate(ALL):
        for move in copies[k]:
            move.wait()

        def planes(group, carry, k=k, slot=slot):
            ratios = []
            for i in range(many):
                p = group * many + i
                if chunk == 0:
                    seen = kept[0][k, p]
                else:
                    seen = jnp.concatenate([kept[0][k, p], kept[1][k, p]], axis=0)
                ratios.append(seen / hold[k, p])
            data = paired(jnp.concatenate(ratios, axis=1), 256)
            section = dot(ayt[chunk, slot], data)
            section = section[:ROWS] + section[ROWS:]
            rows = [section[:, i * QUARTER : (i + 1) * QUARTER] for i in range(many)]
            high, low = halves(jnp.concatenate(rows, axis=0))
            result = dot(jnp.concatenate([high, low], axis=1), wz[slot])
            center = result[:, :128] + result[:, 128:256]
            edge = result[:, 256:384]
            edge = edge + pltpu.roll(edge, 64, 1)
            base = pl.multiple_of(group * (many * SKEW), 8) + k * SLAB * SKEW
            for i in range(many):
                at = base + i * SKEW
                spread[pl.ds(at, ROWS), :] = center[i * ROWS : (i + 1) * ROWS]
                packed = edge[i * ROWS : (i + 1) * ROWS]
                packed = jnp.where(lane < 64, packed[:PACKED], packed[PACKED:])
                spread[pl.ds(at + ROWS, PACKED), :] = packed
            return carry

        lax.fori_loop(0, SLAB // many, planes, 0)

    total = band.shape[1]
    step = 8

    centers = ROWS // step

    def sends(group, edge):
        at = pl.ds(pl.multiple_of(group * step, step), step)
        to = pl.ds(pl.multiple_of((group - edge * centers) * step, step), step)
        return [
            pltpu.make_async_copy(
                totals[k].at[at], outs[3 * edge + k].at[to], out_sems.at[k, group]
            )
            for k in range(3)
        ]

    def some(group, edge):
        at = group * step
        columns = [spread[pl.ds(at + r, n * SLAB, SKEW), :] for r in range(step)]
        result = dot(band[...], paired(jnp.concatenate(columns, axis=1), total))
        result = result[:TALL] + result[TALL:]
        for r in range(step):
            piece = result[:, r * 128 : (r + 1) * 128]
            totals[0][at + r] = piece[:LEFT]
            totals[1][at + r] = piece[LEFT : LEFT + SLAB]
            totals[2][at + r] = piece[LEFT + SLAB :]
        for move in sends(group, edge):
            move.start()
        return edge

    lax.fori_loop(centers, CHUNK // step, lambda group, c: some(group, 1), 1)
    lax.fori_loop(0, centers, lambda group, c: some(group, 0), 0)
    for group in range(CHUNK // step):
        for move in sends(group, int(group >= centers)):
            move.wait()


def adjoint(chunk, spot, band, ayt, wz, forward, recorded, measured, after):
    n = VIEWS
    vmem = pl.BlockSpec(memory_space=pltpu.VMEM)
    hbm = pl.BlockSpec(memory_space=pl.ANY)
    first, last = SPANS[chunk]
    rows = (CUT - first, 128 - CUT)[: chunk + 1]
    sizes = (LEFT, SLAB, RIGHT)
    arrays = [forward]
    for slot in ALL:
        if slot:
            arrays += [measured[piece][slot] for piece in range(chunk + 1)]
        else:
            arrays.append(recorded)
    arrays += after
    return pl.pallas_call(
        lambda *refs: adjoint_kernel(chunk, len(after), *refs),
        out_shape=tuple(shape(r, k, 128) for r in (ROWS, PACKED) for k in sizes),
        in_specs=[pl.BlockSpec(memory_space=pltpu.SMEM)] + [vmem] * 3 + [hbm] * len(arrays),
        out_specs=(hbm,) * 6,
        scratch_shapes=[pltpu.VMEM((n, SLAB, last - first, QUARTER), f32)]
        + [pltpu.VMEM((n, SLAB, k, QUARTER), f32) for k in rows]
        + [pltpu.VMEM((n * SLAB * SKEW + 8, 128), f32)]
        + [pltpu.VMEM((CHUNK, k, 128), f32) for k in sizes]
        + [
            pltpu.SemaphoreType.DMA((n, chunk + 2)),
            pltpu.SemaphoreType.DMA((3, CHUNK // 8)),
        ],
        compiler_params=pltpu.CompilerParams(vmem_limit_bytes=VMEM),
        cost_estimate=pl.CostEstimate(flops=FREE, bytes_accessed=FREE, transcendentals=0),
    )(spot, band, ayt, wz, *arrays)


def added(own, up, down):
    half = SLAB // 2
    whole = own[...] + up[...]
    return whole[:, :half], whole[:, half:] + down[...]


def edges_kernel(own, up, down, *refs):
    rights, lefts = refs[-2:]
    near, far = added(own, up, down)
    lane = lax.broadcasted_iota(jnp.int32, (1, SLAB // 2, 128), 2) % 64
    rights[...] = jnp.where(lane < RIGHT, near, pltpu.roll(far, RIGHT, 2))
    lefts[...] = jnp.where(lane < RIGHT + LEFT, near, pltpu.roll(far, LEFT, 2))


def center_kernel(own, up, down, *refs):
    refs[-1][...] = jnp.concatenate(added(own, up, down), axis=1)


def small(kernel, out_shape, arrays, after, flops):
    vmem = pl.BlockSpec(memory_space=pltpu.VMEM)
    hbm = pl.BlockSpec(memory_space=pl.ANY)
    return pl.pallas_call(
        kernel,
        out_shape=out_shape,
        in_specs=[vmem] * len(arrays) + [hbm] * len(after),
        out_specs=jax.tree.map(lambda _: vmem, out_shape),
        compiler_params=pltpu.CompilerParams(vmem_limit_bytes=VMEM),
        cost_estimate=pl.CostEstimate(flops=flops, bytes_accessed=FREE, transcendentals=0),
    )(*arrays, *after)


def settle_edges(own, up, down, after):
    packed = shape(PACKED, SLAB // 2, 128)
    return small(edges_kernel, (packed, packed), (own, up, down), after, FREE)


def settle_center(own, up, down, after):
    return small(center_kernel, shape(ROWS, SLAB, 128), (own, up, down), after, FREE)


def merge_kernel(center, rights, lefts, *refs):
    out = refs[-1]
    lane = lax.broadcasted_iota(jnp.int32, (SLAB // 2, 128), 1)
    turns = (((0, 64), (96, 32)), ((80, 16), (64, 0)))
    for piece in (0, 1):
        for r in range(PACKED):
            extra = []
            for group in (0, 1):
                low, high = rights[r], lefts[r]
                if turns[0][group][piece]:
                    low = pltpu.roll(low, turns[0][group][piece], 1)
                if turns[1][group][piece]:
                    high = pltpu.roll(high, turns[1][group][piece], 1)
                high = jnp.where(lane >= QUARTER - LEFT, high, 0.0)
                extra.append(jnp.where(lane < RIGHT, low, high))
            at = piece * PACKED + r
            out[:, at, :] = center[at] + jnp.concatenate(extra, axis=0)


def merge(center, rights, lefts, after):
    arrays = (center, rights, lefts)
    return small(merge_kernel, shape(SLAB, ROWS, 128), arrays, after, FREE)


def finish_kernel(count, spot, estimate, *refs):
    out = refs[-1]
    first = 0
    for piece in refs[:count]:
        rows = slice(first, first + piece.shape[1])
        out[:, rows, :] = estimate[:, rows, :] * piece[...] / VIEWS
        first = first + piece.shape[1]


def finish(chunk, step, spot, estimate, pieces, before, after, flops):
    n = 32
    place = pl.BlockSpec(
        (n, ROWS, QUARTER), lambda i, s: (i, chunk, lax.rem(s[0] + (VIEWS - step), VIEWS))
    )
    specs = [place] + [
        pl.BlockSpec((n, piece.shape[1], QUARTER), lambda i, s: (i, 0, 0)) for piece in pieces
    ]
    arrays = [spot, estimate, *pieces]
    aliases = {}
    if before is not None:
        specs.append(pl.BlockSpec(memory_space=pl.ANY))
        arrays.append(before)
        aliases = {len(arrays) - 1: 0}
    arrays += after
    specs += [pl.BlockSpec(memory_space=pl.ANY)] * len(after)
    return call(
        lambda *refs: finish_kernel(len(pieces), *refs),
        shape(*estimate.shape),
        (SLAB // n,),
        specs,
        place,
        prefetch=1,
        aliases=aliases,
        flops=flops,
        moved=FREE,
    )(*arrays)


def along_blk(x, distance):
    size = lax.axis_size("blk")
    route = [(i, i + distance) for i in range(size) if 0 <= i + distance < size]
    return lax.ppermute(x, "blk", route)


def around_view(x, distance):
    return lax.ppermute(x, "view", [(i, (i + distance) % VIEWS) for i in range(VIEWS)])


def along_view(x, distance):
    route = [(i, i + distance) for i in range(VIEWS) if 0 <= i + distance < VIEWS]
    return lax.ppermute(x, "view", route)


def body(estimate, views, psf, offsets):
    q = lax.axis_index("view")
    spot = q[None]
    recorded = views[0]
    middle, last = window(estimate, spot, ())
    upper = along_blk(middle, -1)
    lower = along_blk(last, 1)

    mine = pack(psf[0], offsets[0].astype(f32)[:, None], (middle,))
    params = jnp.stack([mine] + [around_view(mine, s) for s in (1, 2, 3)])
    others = (1, 3, 2)
    pieces = cut(recorded, spot, 0, CUT, others, (params,))
    measured = ({s: around_view(piece, s) for s, piece in zip(others, pieces)}, {})
    starts = params[:, 2, KERN].astype(jnp.int32)
    ax, az, ay, ayt, wz, every = bands(params, pieces)
    forward = forward_of(starts, ax, az, ay, lower, middle, upper)
    pieces = cut(recorded, spot, CUT, 128 - CUT, others, (forward,))
    measured[1].update({s: around_view(piece, s) for s, piece in zip(others, pieces)})

    def spill(parts):
        below, own, above = parts
        return own, along_blk(above, 1), along_blk(below, -1)

    def margins(edges):
        rights, lefts = edges
        return along_view(rights, 1), along_view(lefts, -1)

    def gather(piece):
        left = around_view(piece, 1)
        right = around_view(piece, 3)
        near = around_view(left[:, : ROWS // 2], 1)
        far = around_view(right[:, ROWS // 2 :], 3)
        return piece, left, right, near, far

    def adjoint_of(chunk, after):
        return adjoint(chunk, spot, every, ayt, wz, forward, recorded, measured, after)

    parts0 = adjoint_of(0, pieces)
    spilled0 = spill(parts0[3:]), spill(parts0[:3])
    margins0 = margins(settle_edges(*spilled0[0], (mark((measured[1][1], measured[1][3])),)))
    center0 = settle_center(*spilled0[1], (measured[1][2],))
    piece0 = merge(center0, *margins0, ())
    gathered0 = gather(piece0)
    parts1 = adjoint_of(1, (piece0,))
    spilled1 = spill(parts1[3:]), spill(parts1[:3])
    margins1 = margins(settle_edges(*spilled1[0], gathered0[1:3]))
    center1 = settle_center(*spilled1[1], ())
    piece1 = merge(center1, *margins1, gathered0[3:])
    gathered1 = gather(piece1)
    out = None
    for chunk, gathered in enumerate((gathered0, gathered1)):
        piece, left, right, near, far = gathered
        for step, parts in ((0, (piece,)), (1, (left,)), (3, (right,)), (2, (near, far))):
            after = (piece1,) if out is None else ()
            flops = LONG if (chunk, step) == (1, 1) else FREE
            out = finish(chunk, step, spot, estimate, parts, out, after, flops)
    return out


def solution(mesh):
    placed = (
        P("blk", None, None),
        P("view", "blk", None, None),
        P("view", None, None),
        P("view", None),
    )
    return jax.shard_map(
        body, mesh=mesh, in_specs=placed, out_specs=P("blk", None, None), check_vma=False
    )
```

```python
import jax
import jax.numpy as jnp
from jax import lax
from jax.experimental import pallas as pl
from jax.experimental.pallas import tpu as pltpu
from jax.sharding import PartitionSpec as P

RADIUS = 16
KERN = 33
LEFT = RADIUS
RIGHT = 2 * RADIUS
QUARTER = 128
WIDE = LEFT + QUARTER + RIGHT
SLAB = 32
TALL = LEFT + SLAB + RIGHT
VIEWS = 4
BACKGROUND = 0.1
ALL = (0, 1, 3, 2)
OTHERS = (1, 3, 2)
ROWS = 64
PACKED = ROWS // 2
CHUNK = ROWS + PACKED
CUT = 80
ODD = WIDE + 1
SKEW = CHUNK + 1
FREE = 1 << 10
MICROSECOND = 1 << 30
SPANS = ((0, 80), (32, 128))
VMEM = 48 * 1024 * 1024

f32 = jnp.float32
bf16 = jnp.bfloat16


def call(kernel, out_shape, grid, in_specs, out_specs, prefetch=0, aliases=None, flops=0, moved=0):
    return pl.pallas_call(
        kernel,
        out_shape=out_shape,
        grid_spec=pltpu.PrefetchScalarGridSpec(
            num_scalar_prefetch=prefetch, grid=grid, in_specs=in_specs, out_specs=out_specs
        ),
        input_output_aliases=aliases or {},
        compiler_params=pltpu.CompilerParams(vmem_limit_bytes=VMEM),
        cost_estimate=pl.CostEstimate(flops=flops, bytes_accessed=moved, transcendentals=0),
    )


def shape(*dims, dtype=f32):
    return jax.ShapeDtypeStruct(dims, dtype)


def halves(x):
    high = x.astype(bf16)
    low = (x - high.astype(f32)).astype(bf16)
    return high, low


def stacked(x, axis, blank=0):
    high, low = halves(x)
    parts = [high, low, high]
    if blank:
        dims = list(x.shape)
        dims[axis] = blank
        parts.append(jnp.zeros(dims, bf16))
    return jnp.concatenate(parts, axis=axis)


def paired(x, total):
    high, low = halves(x)
    parts = [high, low]
    if total > 2 * x.shape[0]:
        parts.append(jnp.zeros((total - 2 * x.shape[0], x.shape[1]), bf16))
    return jnp.concatenate(parts, axis=0)


def dot(a, b):
    return lax.dot_general(a, b, (((1,), (0,)), ((), ())), preferred_element_type=f32)


def dot_nt(a, b):
    return lax.dot_general(a, b, (((1,), (1,)), ((), ())), preferred_element_type=f32)


def lag_taps(params, slot, dim, lag):
    value = jnp.zeros(lag.shape, f32)
    for tap in range(KERN):
        value = jnp.where(lag == tap, params[slot, dim, tap], value)
    return value


def thirds(value, part):
    high = value.astype(bf16).astype(f32)
    return jnp.where(part == 2, value - high, high).astype(bf16)


def split(value):
    high = value.astype(bf16).astype(f32)
    return high, value - high


def grid_of(rows, columns):
    return (
        lax.broadcasted_iota(jnp.int32, (rows, columns), 0),
        lax.broadcasted_iota(jnp.int32, (rows, columns), 1),
    )


def spread_band(params, offset, slots, band):
    total = band.shape[1]
    count = SLAB * len(slots)
    row, lane = grid_of(TALL, total)
    part = lane // count
    spot = lane - part * count
    owner = spot // SLAB
    plane = spot - owner * SLAB
    value = jnp.zeros((TALL, total), f32)
    for place, slot in enumerate(slots):
        lag = plane + offset(slot, 0) - row + 2 * RADIUS
        value = jnp.where(owner == place, lag_taps(params, slot, 0, lag), value)
    high, low = split(value)
    band[:TALL, :] = jnp.where(part < 2, high, 0.0).astype(bf16)
    band[TALL:, :] = jnp.where(part < 1, low, 0.0).astype(bf16)


def bands_kernel(params, *refs):
    ax, az, ay, ayt, wz, every = refs[-6:]

    def offset(slot, dim):
        return params[slot, dim, KERN].astype(jnp.int32)

    row, lane = grid_of(SLAB, 256)
    part = lane // TALL
    spot = lane - part * TALL
    for slot in range(VIEWS):
        lag = row + offset(slot, 0) - spot + 2 * RADIUS
        lag = jnp.where(part < 3, lag, -1)
        ax[slot * SLAB : (slot + 1) * SLAB, :] = thirds(lag_taps(params, slot, 0, lag), part)
    row, lane = grid_of(128, 128)
    part = lane // 32
    tail = lane - part * 32 + 128
    edge = lane % 64
    edge = jnp.where(edge < RIGHT, QUARTER + edge, edge - RIGHT - LEFT)
    for slot in range(VIEWS):
        high, low = split(lag_taps(params, slot, 2, row - lane + 2 * RADIUS))
        az[slot, :, 0:128] = high.astype(bf16)
        az[slot, :, 128:256] = high.astype(bf16)
        az[slot, :, 256:384] = low.astype(bf16)
        lag = jnp.where(part < 3, row - tail + 2 * RADIUS, -1)
        az[slot, :, 384:512] = thirds(lag_taps(params, slot, 2, lag), part)
        high, low = split(lag_taps(params, slot, 1, row + offset(slot, 1) - lane + RADIUS))
        ay[slot, :, 0:128] = high.astype(bf16)
        ay[slot, :, 128:256] = high.astype(bf16)
        ay[slot, :, 256:384] = low.astype(bf16)
        high, low = split(lag_taps(params, slot, 2, row + offset(slot, 2) - lane + RADIUS))
        wz[slot, :128, 0:128] = high.astype(bf16)
        wz[slot, 128:, 0:128] = high.astype(bf16)
        wz[slot, :128, 128:256] = low.astype(bf16)
        wz[slot, 128:, 128:256] = jnp.zeros((128, 128), bf16)
        lag = row + offset(slot, 2) - edge + RADIUS
        lag = jnp.where(lane % 64 < RIGHT + LEFT, lag, -1)
        high, low = split(lag_taps(params, slot, 2, lag))
        wz[slot, :128, 256:384] = jnp.where(lane < 64, high, low).astype(bf16)
        wz[slot, 128:, 256:384] = jnp.where(lane < 64, high, 0.0).astype(bf16)
    row, lane = grid_of(ROWS, 256)
    for chunk, (first, last) in enumerate(SPANS):
        count = last - first
        part = lane // count
        spot = first + lane - part * count
        for slot in range(VIEWS):
            lag = spot + offset(slot, 1) - (row + chunk * ROWS) + RADIUS
            high, low = split(lag_taps(params, slot, 1, lag))
            ayt[chunk, slot, :ROWS, :] = jnp.where(part < 2, high, 0.0).astype(bf16)
            ayt[chunk, slot, ROWS:, :] = jnp.where(part < 1, low, 0.0).astype(bf16)
    spread_band(params, offset, ALL, every)


def bands(params, after):
    whole = pl.BlockSpec(memory_space=pltpu.VMEM)
    shapes = (
        shape(VIEWS * SLAB, 256, dtype=bf16),
        shape(VIEWS, QUARTER, 512, dtype=bf16),
        shape(VIEWS, 128, 384, dtype=bf16),
        shape(2, VIEWS, 2 * ROWS, 256, dtype=bf16),
        shape(VIEWS, 256, 384, dtype=bf16),
        shape(2 * TALL, 256, dtype=bf16),
    )
    return pl.pallas_call(
        bands_kernel,
        out_shape=shapes,
        in_specs=[pl.BlockSpec(memory_space=pltpu.SMEM)]
        + [pl.BlockSpec(memory_space=pl.ANY)] * len(after),
        out_specs=(whole,) * len(shapes),
        compiler_params=pltpu.CompilerParams(vmem_limit_bytes=VMEM),
        cost_estimate=pl.CostEstimate(flops=FREE, bytes_accessed=FREE, transcendentals=0),
    )(params, *after)


def pack_kernel(psf, offsets, *refs):
    out = refs[-1]
    taps = psf[...]
    out[:, :KERN] = taps / jnp.sum(taps, axis=1, keepdims=True)
    out[:, KERN:] = offsets[...]


def pack(psf, offsets, after):
    return small(pack_kernel, shape(3, KERN + 1), (psf, offsets), after, FREE)


def mark_kernel(*refs):
    refs[-1][...] = jnp.zeros(refs[-1].shape, f32)


def mark(after, cost):
    return small(mark_kernel, shape(8, 128), (), after, cost * MICROSECOND)


def cut_moves(first, rows, q, recorded, holds, outs, sems):
    reads, writes = [], []
    for k, step in enumerate(OTHERS):
        quarter = lax.rem(q + step, VIEWS)
        lanes = pl.ds(pl.multiple_of(quarter * QUARTER, QUARTER), QUARTER)
        source = recorded.at[:, pl.ds(first, rows), lanes]
        reads.append(pltpu.make_async_copy(source, holds[k], sems.at[0, k]))
        writes.append(pltpu.make_async_copy(holds[k], outs[k], sems.at[1, k]))
    return reads, writes


def cut_shapes(rows):
    return (shape(SLAB, rows, QUARTER),) * len(OTHERS)


def cut_scratch(rows):
    holds = [pltpu.VMEM((SLAB, rows, QUARTER), f32)] * len(OTHERS)
    return holds + [pltpu.SemaphoreType.DMA((2, len(OTHERS)))]


def cut_steps(step, last, reads, writes):
    @pl.when(step == 0)
    def _():
        for move in reads:
            move.start()

    @pl.when(step == 1)
    def _():
        for move, write in zip(reads, writes):
            move.wait()
            write.start()

    def done():
        @pl.when(step == last)
        def _():
            for write in writes:
                write.wait()

    return done


def window_kernel(spot, left, middle, right, recorded, out, low, *refs):
    n = len(OTHERS)
    cuts, flat, holds, sems = refs[:n], refs[n], refs[n + 1 : 2 * n + 1], refs[-1]
    q = spot[0]
    moves = cut_moves(0, CUT, q, recorded, holds, cuts, sems)
    done = cut_steps(pl.program_id(0), SLAB // LEFT - 1, *moves)
    planes = middle.shape[0]
    for i in range(planes):
        before = left[i].T[QUARTER - LEFT :, :]
        after = right[i].T[:RIGHT, :]
        at = i * ODD
        flat[at : at + LEFT, :] = jnp.where(q > 0, before, 0.0)
        flat[at + LEFT : at + LEFT + QUARTER, :] = middle[i].T
        flat[at + LEFT + QUARTER : at + WIDE, :] = jnp.where(q < VIEWS - 1, after, 0.0)
    for z in range(WIDE):
        row = flat[pl.ds(z, planes, ODD), :]
        out[z] = row
        low[z] = row
    done()


def window(estimate, spot, recorded):
    hbm = pl.BlockSpec(memory_space=pl.ANY)
    n = LEFT
    block = (n, 128, QUARTER)
    return pl.pallas_call(
        window_kernel,
        out_shape=(shape(WIDE, SLAB, 128), shape(WIDE, LEFT, 128)) + cut_shapes(CUT),
        grid_spec=pltpu.PrefetchScalarGridSpec(
            num_scalar_prefetch=1,
            grid=(SLAB // n,),
            in_specs=[
                pl.BlockSpec(block, lambda i, s: (i, 0, jnp.maximum(s[0] - 1, 0))),
                pl.BlockSpec(block, lambda i, s: (i, 0, s[0])),
                pl.BlockSpec(block, lambda i, s: (i, 0, jnp.minimum(s[0] + 1, VIEWS - 1))),
                hbm,
            ],
            out_specs=(
                pl.BlockSpec((WIDE, n, 128), lambda i, s: (0, i, 0)),
                pl.BlockSpec((WIDE, n, 128), lambda i, s: (0, 0, 0)),
            )
            + (hbm,) * len(OTHERS),
            scratch_shapes=[pltpu.VMEM((n * ODD + 7, 128), f32)] + cut_scratch(CUT),
        ),
        compiler_params=pltpu.CompilerParams(vmem_limit_bytes=62 * 1024 * 1024),
        cost_estimate=pl.CostEstimate(flops=FREE, bytes_accessed=FREE, transcendentals=0),
    )(spot, estimate, estimate, estimate, recorded)


def forward_kernel(starts, ax, az, ay, lower, middle, upper, recorded, out, *refs):
    n = len(OTHERS)
    cuts, refs = refs[:n], refs[n:]
    blurred, planes_of, load_sems = refs[0], refs[1:4], refs[4]
    holds, sems = refs[5:-1], refs[-1]
    slot = pl.program_id(0)
    moves = cut_moves(CUT, 128 - CUT, starts[VIEWS], recorded, holds, cuts, sems)
    done = cut_steps(slot, VIEWS - 1, *moves)
    step = 16

    def loads(group):
        at = pl.ds(pl.multiple_of(group * step, step), step)
        return [
            pltpu.make_async_copy(ref.at[at], planes_of[k].at[at], load_sems.at[k, group])
            for k, ref in enumerate((lower, middle, upper))
        ]

    @pl.when(slot == 0)
    def _():
        for group in range(WIDE // step):
            for move in loads(group):
                move.start()

        def some(group, carry):
            for move in loads(group):
                move.wait()
            at = group * step
            columns = [
                jnp.concatenate([ref[at + z] for ref in planes_of], axis=0) for z in range(step)
            ]
            data = stacked(jnp.concatenate(columns, axis=1), 0, 256 - 3 * TALL)
            result = dot(ax[...], data)
            for z in range(step):
                blurred[pl.ds(at + z, VIEWS * SLAB, ODD), :] = result[:, z * 128 : z * 128 + 128]
            return carry

        lax.fori_loop(0, WIDE // step, some, 0)

    start = starts[slot]
    span = QUARTER + 2 * RADIUS
    many = SLAB

    def planes(group, carry):
        first = slot * SLAB + group * many
        data = jnp.concatenate(
            [blurred[pl.ds((first + i) * ODD + start, span), :] for i in range(many)], axis=1
        )
        high, low = halves(data)
        blank = jnp.zeros((32, many * 128), bf16)
        data = [high[:128], low[:128], high[:128], high[128:], low[128:], high[128:], blank]
        section = dot(az[0], jnp.concatenate(data, axis=0))
        section = jnp.concatenate([section[:, i * 128 : i * 128 + 128] for i in range(many)], axis=0)
        result = dot_nt(ay[0], stacked(section, 1)) + BACKGROUND
        for i in range(many):
            out[group * many + i] = result[:, i * QUARTER : (i + 1) * QUARTER]
        return carry

    lax.fori_loop(0, SLAB // many, planes, 0)
    done()


def forward_of(starts, ax, az, ay, lower, middle, upper, recorded):
    hbm = pl.BlockSpec(memory_space=pl.ANY)
    rows = 128 - CUT

    def once(x):
        return pl.BlockSpec(x.shape, lambda v, s: (0,) * x.ndim, pipeline_mode=pl.Buffered(1))

    return pl.pallas_call(
        forward_kernel,
        out_shape=(shape(VIEWS * SLAB, 128, QUARTER),) + cut_shapes(rows),
        grid_spec=pltpu.PrefetchScalarGridSpec(
            num_scalar_prefetch=1,
            grid=(VIEWS,),
            in_specs=[
                once(ax),
                pl.BlockSpec((1,) + az.shape[1:], lambda v, s: (v, 0, 0)),
                pl.BlockSpec((1,) + ay.shape[1:], lambda v, s: (v, 0, 0)),
                hbm,
                hbm,
                hbm,
                hbm,
            ],
            out_specs=(pl.BlockSpec((SLAB, 128, QUARTER), lambda v, s: (v, 0, 0)),)
            + (hbm,) * len(OTHERS),
            scratch_shapes=[pltpu.VMEM((VIEWS * SLAB * ODD + 8, 128), f32)]
            + [pltpu.VMEM(x.shape, f32) for x in (lower, middle, upper)]
            + [pltpu.SemaphoreType.DMA((3, WIDE // 16))]
            + cut_scratch(rows),
        ),
        compiler_params=pltpu.CompilerParams(vmem_limit_bytes=VMEM),
        cost_estimate=pl.CostEstimate(flops=FREE, bytes_accessed=FREE, transcendentals=0),
    )(starts, ax, az, ay, lower, middle, upper, recorded)


def adjoint_kernel(chunk, extra, *refs):
    n = VIEWS
    pieces = chunk + 1
    first, last = SPANS[chunk]
    bounds = ((first, CUT), (CUT, 128))[:pieces]
    spot, band, ayt, wz, forward = refs[:5]
    refs = list(refs[5:])
    measured = []
    for slot in ALL:
        if slot == 0:
            lanes = pl.ds(pl.multiple_of(spot[0] * QUARTER, QUARTER), QUARTER)
            whole = refs.pop(0)
            measured.append([whole.at[:, pl.ds(a, b - a), lanes] for a, b in bounds])
        else:
            measured.append([refs.pop(0).at[:, pl.ds(first, CUT - first), :]])
            if chunk:
                measured[-1].append(refs.pop(0))
    refs = refs[extra:]
    outs, refs = refs[:5], refs[5:]
    hold, kept, spread = refs[0], refs[1 : 1 + pieces], refs[1 + pieces]
    totals = refs[2 + pieces : 5 + pieces]
    sems, out_sems = refs[-2:]
    copies = []
    for k, slot in enumerate(ALL):
        source = forward.at[pl.ds(slot * SLAB, SLAB), pl.ds(first, last - first), :]
        moves = [pltpu.make_async_copy(source, hold.at[k], sems.at[k, 0])]
        for piece in range(pieces):
            target = kept[piece].at[k]
            moves.append(pltpu.make_async_copy(measured[k][piece], target, sems.at[k, 1 + piece]))
        for move in moves:
            move.start()
        copies.append(moves)

    many = SLAB
    lane = lax.broadcasted_iota(jnp.int32, (PACKED, 128), 1)
    for k, slot in enumerate(ALL):
        for move in copies[k]:
            move.wait()

        def planes(group, carry, k=k, slot=slot):
            ratios = []
            for i in range(many):
                p = group * many + i
                if chunk == 0:
                    seen = kept[0][k, p]
                else:
                    seen = jnp.concatenate([kept[0][k, p], kept[1][k, p]], axis=0)
                ratios.append(seen / hold[k, p])
            data = paired(jnp.concatenate(ratios, axis=1), 256)
            section = dot(ayt[chunk, slot], data)
            section = section[:ROWS] + section[ROWS:]
            rows = [section[:, i * QUARTER : (i + 1) * QUARTER] for i in range(many)]
            high, low = halves(jnp.concatenate(rows, axis=0))
            result = dot(jnp.concatenate([high, low], axis=1), wz[slot])
            center = result[:, :128] + result[:, 128:256]
            edge = result[:, 256:384]
            edge = edge + pltpu.roll(edge, 64, 1)
            base = pl.multiple_of(group * (many * SKEW), 8) + k * SLAB * SKEW
            for i in range(many):
                at = base + i * SKEW
                spread[pl.ds(at, ROWS), :] = center[i * ROWS : (i + 1) * ROWS]
                packed = edge[i * ROWS : (i + 1) * ROWS]
                packed = jnp.where(lane < 64, packed[:PACKED], packed[PACKED:])
                spread[pl.ds(at + ROWS, PACKED), :] = packed
            return carry

        lax.fori_loop(0, SLAB // many, planes, 0)

    total = band.shape[1]
    step = 32

    centers = ROWS // step

    def sends(group, edge):
        at = pl.ds(pl.multiple_of(group * step, step), step)
        to = pl.ds(pl.multiple_of((group - edge * centers) * step, step), step)
        targets = outs[0].at[at], outs[1 + 2 * edge].at[to], outs[2 + 2 * edge].at[to]
        return [
            pltpu.make_async_copy(totals[k].at[at], targets[k], out_sems.at[k, group])
            for k in range(3)
        ]

    def some(group, edge):
        at = group * step
        columns = [spread[pl.ds(at + r, n * SLAB, SKEW), :] for r in range(step)]
        result = dot(band[...], paired(jnp.concatenate(columns, axis=1), total))
        result = result[:TALL] + result[TALL:]
        for r in range(step):
            piece = result[:, r * 128 : (r + 1) * 128]
            totals[0][at + r] = piece[:LEFT]
            totals[1][at + r] = piece[LEFT : LEFT + SLAB]
            totals[2][at + r] = piece[LEFT + SLAB :]
        for move in sends(group, edge):
            move.start()
        return edge

    lax.fori_loop(centers, CHUNK // step, lambda group, c: some(group, 1), 1)
    lax.fori_loop(0, centers, lambda group, c: some(group, 0), 0)
    for group in range(CHUNK // step):
        for move in sends(group, int(group >= centers)):
            move.wait()


def adjoint(chunk, spot, band, ayt, wz, forward, recorded, measured, after):
    n = VIEWS
    vmem = pl.BlockSpec(memory_space=pltpu.VMEM)
    hbm = pl.BlockSpec(memory_space=pl.ANY)
    first, last = SPANS[chunk]
    rows = (CUT - first, 128 - CUT)[: chunk + 1]
    sizes = (LEFT, SLAB, RIGHT)
    arrays = [forward]
    for slot in ALL:
        if slot:
            arrays += [measured[piece][slot] for piece in range(chunk + 1)]
        else:
            arrays.append(recorded)
    arrays += after
    return pl.pallas_call(
        lambda *refs: adjoint_kernel(chunk, len(after), *refs),
        out_shape=(shape(CHUNK, LEFT, 128),)
        + tuple(shape(r, k, 128) for r in (ROWS, PACKED) for k in sizes[1:]),
        in_specs=[pl.BlockSpec(memory_space=pltpu.SMEM)] + [vmem] * 3 + [hbm] * len(arrays),
        out_specs=(hbm,) * 5,
        scratch_shapes=[pltpu.VMEM((n, SLAB, last - first, QUARTER), f32)]
        + [pltpu.VMEM((n, SLAB, k, QUARTER), f32) for k in rows]
        + [pltpu.VMEM((n * SLAB * SKEW + 8, 128), f32)]
        + [pltpu.VMEM((CHUNK, k, 128), f32) for k in sizes]
        + [
            pltpu.SemaphoreType.DMA((n, chunk + 2)),
            pltpu.SemaphoreType.DMA((3, CHUNK // 32)),
        ],
        compiler_params=pltpu.CompilerParams(vmem_limit_bytes=VMEM),
        cost_estimate=pl.CostEstimate(flops=FREE, bytes_accessed=FREE, transcendentals=0),
    )(spot, band, ayt, wz, *arrays)


def added(own, up, down):
    half = SLAB // 2
    whole = own[...] + up[...]
    return whole[:, :half], whole[:, half:] + down


def edges_kernel(own, up, down, *refs):
    rights, lefts = refs[-2:]
    near, far = added(own, up, down[ROWS:])
    lane = lax.broadcasted_iota(jnp.int32, (1, SLAB // 2, 128), 2) % 64
    rights[...] = jnp.where(lane < RIGHT, near, pltpu.roll(far, RIGHT, 2))
    lefts[...] = jnp.where(lane < RIGHT + LEFT, near, pltpu.roll(far, LEFT, 2))


def center_kernel(own, up, down, *refs):
    refs[-1][...] = jnp.concatenate(added(own, up, down[:ROWS]), axis=1)


def small(kernel, out_shape, arrays, after, flops):
    vmem = pl.BlockSpec(memory_space=pltpu.VMEM)
    hbm = pl.BlockSpec(memory_space=pl.ANY)
    return pl.pallas_call(
        kernel,
        out_shape=out_shape,
        in_specs=[vmem] * len(arrays) + [hbm] * len(after),
        out_specs=jax.tree.map(lambda _: vmem, out_shape),
        compiler_params=pltpu.CompilerParams(vmem_limit_bytes=VMEM),
        cost_estimate=pl.CostEstimate(flops=flops, bytes_accessed=FREE, transcendentals=0),
    )(*arrays, *after)


def settle_edges(own, up, down, after):
    packed = shape(PACKED, SLAB // 2, 128)
    return small(edges_kernel, (packed, packed), (own, up, down), after, 5 * MICROSECOND)


def settle_center(own, up, down, after):
    return small(center_kernel, shape(ROWS, SLAB, 128), (own, up, down), after, FREE)


def merge_kernel(center, rights, lefts, *refs):
    lane = lax.broadcasted_iota(jnp.int32, (SLAB // 2, 128), 1)
    turns = (((0, 64), (96, 32)), ((80, 16), (64, 0)))
    for piece in (0, 1):
        for r in range(PACKED):
            extra = []
            for group in (0, 1):
                low, high = rights[r], lefts[r]
                if turns[0][group][piece]:
                    low = pltpu.roll(low, turns[0][group][piece], 1)
                if turns[1][group][piece]:
                    high = pltpu.roll(high, turns[1][group][piece], 1)
                high = jnp.where(lane >= QUARTER - LEFT, high, 0.0)
                extra.append(jnp.where(lane < RIGHT, low, high))
            at = piece * PACKED + r
            refs[piece - 2][:, r, :] = center[at] + jnp.concatenate(extra, axis=0)


def merge(center, rights, lefts, after):
    arrays = (center, rights, lefts)
    return small(merge_kernel, (shape(SLAB, PACKED, 128),) * 2, arrays, after, FREE)


def finish_kernel(count, spot, estimate, *refs):
    out = refs[-1]
    first = 0
    for piece in refs[:count]:
        rows = slice(first, first + piece.shape[1])
        out[:, rows, :] = estimate[:, rows, :] * piece[...] / VIEWS
        first = first + piece.shape[1]


def finish(chunk, step, spot, estimate, pieces, before, after):
    n = 32
    place = pl.BlockSpec(
        (n, ROWS, QUARTER), lambda i, s: (i, chunk, lax.rem(s[0] + (VIEWS - step), VIEWS))
    )
    specs = [place] + [
        pl.BlockSpec((n, piece.shape[1], QUARTER), lambda i, s: (i, 0, 0)) for piece in pieces
    ]
    arrays = [spot, estimate, *pieces]
    aliases = {}
    if before is not None:
        specs.append(pl.BlockSpec(memory_space=pl.ANY))
        arrays.append(before)
        aliases = {len(arrays) - 1: 0}
    arrays += after
    specs += [pl.BlockSpec(memory_space=pl.ANY)] * len(after)
    return call(
        lambda *refs: finish_kernel(len(pieces), *refs),
        shape(*estimate.shape),
        (SLAB // n,),
        specs,
        place,
        prefetch=1,
        aliases=aliases,
        flops=FREE,
        moved=FREE,
    )(*arrays)


def along_blk(x, distance):
    size = lax.axis_size("blk")
    route = [(i, i + distance) for i in range(size) if 0 <= i + distance < size]
    return lax.ppermute(x, "blk", route)


def around_view(x, distance):
    return lax.ppermute(x, "view", [(i, (i + distance) % VIEWS) for i in range(VIEWS)])


def along_view(x, distance):
    route = [(i, i + distance) for i in range(VIEWS) if 0 <= i + distance < VIEWS]
    return lax.ppermute(x, "view", route)


def body(estimate, views, psf, offsets):
    q = lax.axis_index("view")
    spot = q[None]
    recorded = views[0]
    middle, last, *pieces = window(estimate, spot, recorded)
    upper = along_blk(middle, -1)
    lower = along_blk(last, 1)

    mine = pack(psf[0], offsets[0].astype(f32)[:, None], (middle,))
    params = jnp.stack([mine] + [around_view(mine, s) for s in (1, 2, 3)])
    measured = ({s: around_view(piece, s) for s, piece in zip(OTHERS, pieces)}, {})
    starts = jnp.concatenate([params[:, 2, KERN].astype(jnp.int32), spot])
    ax, az, ay, ayt, wz, every = bands(params, ())
    forward, *pieces = forward_of(starts, ax, az, ay, lower, middle, upper, recorded)
    measured[1].update({s: around_view(piece, s) for s, piece in zip(OTHERS, pieces)})

    def spill(parts):
        below, own, above, own_edge, above_edge = parts
        down = along_blk(below, -1)
        return (own_edge, along_blk(above_edge, 1), down), (own, along_blk(above, 1), down)

    def margins(edges):
        rights, lefts = edges
        return along_view(rights, 1), along_view(lefts, -1)

    def gather(piece):
        near, far = piece
        left = around_view(near, 1), around_view(far, 1)
        right = around_view(near, 3), around_view(far, 3)
        opposite = around_view(left[0], 1), around_view(right[1], 3)
        return piece, left, right, opposite

    def adjoint_of(chunk, after):
        return adjoint(chunk, spot, every, ayt, wz, forward, recorded, measured, after)

    parts0 = adjoint_of(0, ())
    spilled0 = spill(parts0)
    margins0 = margins(settle_edges(*spilled0[0], (mark((measured[1][1], measured[1][3]), 16),)))
    center0 = settle_center(*spilled0[1], (measured[1][2],))
    piece0 = merge(center0, *margins0, ())
    gathered0 = gather(piece0)
    parts1 = adjoint_of(1, tuple(piece0))
    spilled1 = spill(parts1)
    margins1 = margins(settle_edges(*spilled1[0], (mark((gathered0[1][0], gathered0[2][1]), 8),)))
    center1 = settle_center(*spilled1[1], ())
    piece1 = merge(center1, *margins1, gathered0[3] + (gathered0[1][1], gathered0[2][0]))
    gathered1 = gather(piece1)
    out = None
    for chunk, gathered in enumerate((gathered0, gathered1)):
        for step, parts in zip((0, 1, 3, 2), gathered):
            after = () if out is not None else (gathered1[1][0], gathered1[2][1])
            out = finish(chunk, step, spot, estimate, parts, out, after)
    return out


def solution(mesh):
    placed = (
        P("blk", None, None),
        P("view", "blk", None, None),
        P("view", None, None),
        P("view", None),
    )
    return jax.shard_map(
        body, mesh=mesh, in_specs=placed, out_specs=P("blk", None, None), check_vma=False
    )
```

```python
import jax
import jax.numpy as jnp
from jax import lax
from jax.experimental import pallas as pl
from jax.experimental.pallas import tpu as pltpu
from jax.sharding import PartitionSpec as P

RADIUS = 16
KERN = 33
LEFT = RADIUS
RIGHT = 2 * RADIUS
QUARTER = 128
WIDE = LEFT + QUARTER + RIGHT
SLAB = 32
TALL = LEFT + SLAB + RIGHT
VIEWS = 4
BACKGROUND = 0.1
ALL = (0, 1, 3, 2)
OTHERS = (1, 3, 2)
ROWS = 64
PACKED = ROWS // 2
CHUNK = ROWS + PACKED
CUT = 80
ODD = WIDE + 1
SKEW = CHUNK + 1
FREE = 1 << 10
MICROSECOND = 1 << 30
SPANS = ((0, 80), (32, 128))
VMEM = 48 * 1024 * 1024

f32 = jnp.float32
bf16 = jnp.bfloat16


def call(kernel, out_shape, grid, in_specs, out_specs, prefetch=0, aliases=None, flops=0, moved=0):
    return pl.pallas_call(
        kernel,
        out_shape=out_shape,
        grid_spec=pltpu.PrefetchScalarGridSpec(
            num_scalar_prefetch=prefetch, grid=grid, in_specs=in_specs, out_specs=out_specs
        ),
        input_output_aliases=aliases or {},
        compiler_params=pltpu.CompilerParams(vmem_limit_bytes=VMEM),
        cost_estimate=pl.CostEstimate(flops=flops, bytes_accessed=moved, transcendentals=0),
    )


def shape(*dims, dtype=f32):
    return jax.ShapeDtypeStruct(dims, dtype)


def halves(x):
    high = x.astype(bf16)
    low = (x - high.astype(f32)).astype(bf16)
    return high, low


def stacked(x, axis, blank=0):
    high, low = halves(x)
    parts = [high, low, high]
    if blank:
        dims = list(x.shape)
        dims[axis] = blank
        parts.append(jnp.zeros(dims, bf16))
    return jnp.concatenate(parts, axis=axis)


def paired(x, total):
    high, low = halves(x)
    parts = [high, low]
    if total > 2 * x.shape[0]:
        parts.append(jnp.zeros((total - 2 * x.shape[0], x.shape[1]), bf16))
    return jnp.concatenate(parts, axis=0)


def dot(a, b):
    return lax.dot_general(a, b, (((1,), (0,)), ((), ())), preferred_element_type=f32)


def dot_nt(a, b):
    return lax.dot_general(a, b, (((1,), (1,)), ((), ())), preferred_element_type=f32)


def lag_taps(params, slot, dim, lag):
    value = jnp.zeros(lag.shape, f32)
    for tap in range(KERN):
        value = jnp.where(lag == tap, params[slot, dim, tap], value)
    return value


def thirds(value, part):
    high = value.astype(bf16).astype(f32)
    return jnp.where(part == 2, value - high, high).astype(bf16)


def split(value):
    high = value.astype(bf16).astype(f32)
    return high, value - high


def grid_of(rows, columns):
    return (
        lax.broadcasted_iota(jnp.int32, (rows, columns), 0),
        lax.broadcasted_iota(jnp.int32, (rows, columns), 1),
    )


def spread_band(params, offset, slots, band):
    total = band.shape[1]
    count = SLAB * len(slots)
    row, lane = grid_of(TALL, total)
    part = lane // count
    spot = lane - part * count
    owner = spot // SLAB
    plane = spot - owner * SLAB
    value = jnp.zeros((TALL, total), f32)
    for place, slot in enumerate(slots):
        lag = plane + offset(slot, 0) - row + 2 * RADIUS
        value = jnp.where(owner == place, lag_taps(params, slot, 0, lag), value)
    high, low = split(value)
    band[:TALL, :] = jnp.where(part < 2, high, 0.0).astype(bf16)
    band[TALL:, :] = jnp.where(part < 1, low, 0.0).astype(bf16)


def bands_kernel(params, *refs):
    ax, az, ay, ayt, wz, every = refs[-6:]

    def offset(slot, dim):
        return params[slot, dim, KERN].astype(jnp.int32)

    row, lane = grid_of(SLAB, 256)
    part = lane // TALL
    spot = lane - part * TALL
    for slot in range(VIEWS):
        lag = row + offset(slot, 0) - spot + 2 * RADIUS
        lag = jnp.where(part < 3, lag, -1)
        ax[slot * SLAB : (slot + 1) * SLAB, :] = thirds(lag_taps(params, slot, 0, lag), part)
    row, lane = grid_of(128, 128)
    part = lane // 32
    tail = lane - part * 32 + 128
    edge = lane % 64
    edge = jnp.where(edge < RIGHT, QUARTER + edge, edge - RIGHT - LEFT)
    for slot in range(VIEWS):
        high, low = split(lag_taps(params, slot, 2, row - lane + 2 * RADIUS))
        az[slot, :, 0:128] = high.astype(bf16)
        az[slot, :, 128:256] = high.astype(bf16)
        az[slot, :, 256:384] = low.astype(bf16)
        lag = jnp.where(part < 3, row - tail + 2 * RADIUS, -1)
        az[slot, :, 384:512] = thirds(lag_taps(params, slot, 2, lag), part)
        high, low = split(lag_taps(params, slot, 1, row + offset(slot, 1) - lane + RADIUS))
        ay[slot, :, 0:128] = high.astype(bf16)
        ay[slot, :, 128:256] = high.astype(bf16)
        ay[slot, :, 256:384] = low.astype(bf16)
        high, low = split(lag_taps(params, slot, 2, row + offset(slot, 2) - lane + RADIUS))
        wz[slot, :128, 0:128] = high.astype(bf16)
        wz[slot, 128:, 0:128] = high.astype(bf16)
        wz[slot, :128, 128:256] = low.astype(bf16)
        wz[slot, 128:, 128:256] = jnp.zeros((128, 128), bf16)
        lag = row + offset(slot, 2) - edge + RADIUS
        lag = jnp.where(lane % 64 < RIGHT + LEFT, lag, -1)
        high, low = split(lag_taps(params, slot, 2, lag))
        wz[slot, :128, 256:384] = jnp.where(lane < 64, high, low).astype(bf16)
        wz[slot, 128:, 256:384] = jnp.where(lane < 64, high, 0.0).astype(bf16)
    row, lane = grid_of(ROWS, 256)
    for chunk, (first, last) in enumerate(SPANS):
        count = last - first
        part = lane // count
        spot = first + lane - part * count
        for slot in range(VIEWS):
            lag = spot + offset(slot, 1) - (row + chunk * ROWS) + RADIUS
            high, low = split(lag_taps(params, slot, 1, lag))
            ayt[chunk, slot, :ROWS, :] = jnp.where(part < 2, high, 0.0).astype(bf16)
            ayt[chunk, slot, ROWS:, :] = jnp.where(part < 1, low, 0.0).astype(bf16)
    spread_band(params, offset, ALL, every)


def bands(params, after):
    whole = pl.BlockSpec(memory_space=pltpu.VMEM)
    shapes = (
        shape(VIEWS * SLAB, 256, dtype=bf16),
        shape(VIEWS, QUARTER, 512, dtype=bf16),
        shape(VIEWS, 128, 384, dtype=bf16),
        shape(2, VIEWS, 2 * ROWS, 256, dtype=bf16),
        shape(VIEWS, 256, 384, dtype=bf16),
        shape(2 * TALL, 256, dtype=bf16),
    )
    return pl.pallas_call(
        bands_kernel,
        out_shape=shapes,
        in_specs=[pl.BlockSpec(memory_space=pltpu.SMEM)]
        + [pl.BlockSpec(memory_space=pl.ANY)] * len(after),
        out_specs=(whole,) * len(shapes),
        compiler_params=pltpu.CompilerParams(vmem_limit_bytes=VMEM),
        cost_estimate=pl.CostEstimate(flops=FREE, bytes_accessed=FREE, transcendentals=0),
    )(params, *after)


def pack_kernel(psf, offsets, *refs):
    out = refs[-1]
    taps = psf[...]
    out[:, :KERN] = taps / jnp.sum(taps, axis=1, keepdims=True)
    out[:, KERN:] = offsets[...]


def pack(psf, offsets, after):
    return small(pack_kernel, shape(3, KERN + 1), (psf, offsets), after, FREE)


def mark_kernel(*refs):
    refs[-1][...] = jnp.zeros(refs[-1].shape, f32)


def mark(after, cost):
    return small(mark_kernel, shape(8, 128), (), after, cost * MICROSECOND)


def cut_moves(first, rows, q, recorded, holds, outs, sems):
    reads, writes = [], []
    for k, step in enumerate(OTHERS):
        quarter = lax.rem(q + step, VIEWS)
        lanes = pl.ds(pl.multiple_of(quarter * QUARTER, QUARTER), QUARTER)
        source = recorded.at[:, pl.ds(first, rows), lanes]
        reads.append(pltpu.make_async_copy(source, holds[k], sems.at[0, k]))
        writes.append(pltpu.make_async_copy(holds[k], outs[k], sems.at[1, k]))
    return reads, writes


def cut_shapes(rows):
    return (shape(SLAB, rows, QUARTER),) * len(OTHERS)


def cut_scratch(rows):
    holds = [pltpu.VMEM((SLAB, rows, QUARTER), f32)] * len(OTHERS)
    return holds + [pltpu.SemaphoreType.DMA((2, len(OTHERS)))]


def cut_steps(step, last, reads, writes):
    @pl.when(step == 0)
    def _():
        for move in reads:
            move.start()

    @pl.when(step == 1)
    def _():
        for move, write in zip(reads, writes):
            move.wait()
            write.start()

    def done():
        @pl.when(step == last)
        def _():
            for write in writes:
                write.wait()

    return done


def window_kernel(spot, left, middle, right, recorded, out, low, token, *refs):
    token[...] = jnp.zeros(token.shape, f32)
    n = len(OTHERS)
    cuts, flat, holds, sems = refs[:n], refs[n], refs[n + 1 : 2 * n + 1], refs[-1]
    q = spot[0]
    moves = cut_moves(0, CUT, q, recorded, holds, cuts, sems)
    done = cut_steps(pl.program_id(0), SLAB // LEFT - 1, *moves)
    planes = middle.shape[0]
    for i in range(planes):
        before = left[i].T[QUARTER - LEFT :, :]
        after = right[i].T[:RIGHT, :]
        at = i * ODD
        flat[at : at + LEFT, :] = jnp.where(q > 0, before, 0.0)
        flat[at + LEFT : at + LEFT + QUARTER, :] = middle[i].T
        flat[at + LEFT + QUARTER : at + WIDE, :] = jnp.where(q < VIEWS - 1, after, 0.0)
    for z in range(WIDE):
        row = flat[pl.ds(z, planes, ODD), :]
        out[z] = row
        low[z] = row
    done()


def window(estimate, spot, recorded):
    hbm = pl.BlockSpec(memory_space=pl.ANY)
    n = LEFT
    block = (n, 128, QUARTER)
    return pl.pallas_call(
        window_kernel,
        out_shape=(shape(WIDE, SLAB, 128), shape(WIDE, LEFT, 128), shape(8, 128))
        + cut_shapes(CUT),
        grid_spec=pltpu.PrefetchScalarGridSpec(
            num_scalar_prefetch=1,
            grid=(SLAB // n,),
            in_specs=[
                pl.BlockSpec(block, lambda i, s: (i, 0, jnp.maximum(s[0] - 1, 0))),
                pl.BlockSpec(block, lambda i, s: (i, 0, s[0])),
                pl.BlockSpec(block, lambda i, s: (i, 0, jnp.minimum(s[0] + 1, VIEWS - 1))),
                hbm,
            ],
            out_specs=(
                pl.BlockSpec((WIDE, n, 128), lambda i, s: (0, i, 0)),
                pl.BlockSpec((WIDE, n, 128), lambda i, s: (0, 0, 0)),
                pl.BlockSpec((8, 128), lambda i, s: (0, 0)),
            )
            + (hbm,) * len(OTHERS),
            scratch_shapes=[pltpu.VMEM((n * ODD + 7, 128), f32)] + cut_scratch(CUT),
        ),
        compiler_params=pltpu.CompilerParams(vmem_limit_bytes=62 * 1024 * 1024),
        cost_estimate=pl.CostEstimate(flops=FREE, bytes_accessed=FREE, transcendentals=0),
    )(spot, estimate, estimate, estimate, recorded)


def forward_kernel(starts, ax, az, ay, lower, middle, upper, recorded, out, *refs):
    n = len(OTHERS)
    cuts, refs = refs[:n], refs[n:]
    blurred, planes_of, load_sems = refs[0], refs[1:4], refs[4]
    holds, sems = refs[5:-1], refs[-1]
    slot = pl.program_id(0)
    moves = cut_moves(CUT, 128 - CUT, starts[VIEWS], recorded, holds, cuts, sems)
    done = cut_steps(slot, VIEWS - 1, *moves)
    step = 16

    def loads(group):
        at = pl.ds(pl.multiple_of(group * step, step), step)
        return [
            pltpu.make_async_copy(ref.at[at], planes_of[k].at[at], load_sems.at[k, group])
            for k, ref in enumerate((lower, middle, upper))
        ]

    @pl.when(slot == 0)
    def _():
        for group in range(WIDE // step):
            for move in loads(group):
                move.start()

        def some(group, carry):
            for move in loads(group):
                move.wait()
            at = group * step
            columns = [
                jnp.concatenate([ref[at + z] for ref in planes_of], axis=0) for z in range(step)
            ]
            data = stacked(jnp.concatenate(columns, axis=1), 0, 256 - 3 * TALL)
            result = dot(ax[...], data)
            for z in range(step):
                blurred[pl.ds(at + z, VIEWS * SLAB, ODD), :] = result[:, z * 128 : z * 128 + 128]
            return carry

        lax.fori_loop(0, WIDE // step, some, 0)

    start = starts[slot]
    span = QUARTER + 2 * RADIUS
    many = SLAB

    def planes(group, carry):
        first = slot * SLAB + group * many
        data = jnp.concatenate(
            [blurred[pl.ds((first + i) * ODD + start, span), :] for i in range(many)], axis=1
        )
        high, low = halves(data)
        blank = jnp.zeros((32, many * 128), bf16)
        data = [high[:128], low[:128], high[:128], high[128:], low[128:], high[128:], blank]
        section = dot(az[0], jnp.concatenate(data, axis=0))
        section = jnp.concatenate([section[:, i * 128 : i * 128 + 128] for i in range(many)], axis=0)
        result = dot_nt(ay[0], stacked(section, 1)) + BACKGROUND
        for i in range(many):
            out[group * many + i] = result[:, i * QUARTER : (i + 1) * QUARTER]
        return carry

    lax.fori_loop(0, SLAB // many, planes, 0)
    done()


def forward_of(starts, ax, az, ay, lower, middle, upper, recorded):
    hbm = pl.BlockSpec(memory_space=pl.ANY)
    rows = 128 - CUT

    def once(x):
        return pl.BlockSpec(x.shape, lambda v, s: (0,) * x.ndim, pipeline_mode=pl.Buffered(1))

    return pl.pallas_call(
        forward_kernel,
        out_shape=(shape(VIEWS * SLAB, 128, QUARTER),) + cut_shapes(rows),
        grid_spec=pltpu.PrefetchScalarGridSpec(
            num_scalar_prefetch=1,
            grid=(VIEWS,),
            in_specs=[
                once(ax),
                pl.BlockSpec((1,) + az.shape[1:], lambda v, s: (v, 0, 0)),
                pl.BlockSpec((1,) + ay.shape[1:], lambda v, s: (v, 0, 0)),
                hbm,
                hbm,
                hbm,
                hbm,
            ],
            out_specs=(pl.BlockSpec((SLAB, 128, QUARTER), lambda v, s: (v, 0, 0)),)
            + (hbm,) * len(OTHERS),
            scratch_shapes=[pltpu.VMEM((VIEWS * SLAB * ODD + 8, 128), f32)]
            + [pltpu.VMEM(x.shape, f32) for x in (lower, middle, upper)]
            + [pltpu.SemaphoreType.DMA((3, WIDE // 16))]
            + cut_scratch(rows),
        ),
        compiler_params=pltpu.CompilerParams(vmem_limit_bytes=VMEM),
        cost_estimate=pl.CostEstimate(flops=FREE, bytes_accessed=FREE, transcendentals=0),
    )(starts, ax, az, ay, lower, middle, upper, recorded)


def adjoint_kernel(chunk, extra, *refs):
    n = VIEWS
    pieces = chunk + 1
    first, last = SPANS[chunk]
    bounds = ((first, CUT), (CUT, 128))[:pieces]
    spot, band, ayt, wz, forward = refs[:5]
    refs = list(refs[5:])
    measured = []
    for slot in ALL:
        if slot == 0:
            lanes = pl.ds(pl.multiple_of(spot[0] * QUARTER, QUARTER), QUARTER)
            whole = refs.pop(0)
            measured.append([whole.at[:, pl.ds(a, b - a), lanes] for a, b in bounds])
        else:
            measured.append([refs.pop(0).at[:, pl.ds(first, CUT - first), :]])
            if chunk:
                measured[-1].append(refs.pop(0))
    refs = refs[extra:]
    outs, refs = refs[:5], refs[5:]
    hold, kept, spread = refs[0], refs[1 : 1 + pieces], refs[1 + pieces]
    totals = refs[2 + pieces : 5 + pieces]
    sems, out_sems = refs[-2:]
    copies = []
    for k, slot in enumerate(ALL):
        source = forward.at[pl.ds(slot * SLAB, SLAB), pl.ds(first, last - first), :]
        moves = [pltpu.make_async_copy(source, hold.at[k], sems.at[k, 0])]
        for piece in range(pieces):
            target = kept[piece].at[k]
            moves.append(pltpu.make_async_copy(measured[k][piece], target, sems.at[k, 1 + piece]))
        for move in moves:
            move.start()
        copies.append(moves)

    many = SLAB
    lane = lax.broadcasted_iota(jnp.int32, (PACKED, 128), 1)
    for k, slot in enumerate(ALL):
        for move in copies[k]:
            move.wait()

        def planes(group, carry, k=k, slot=slot):
            ratios = []
            for i in range(many):
                p = group * many + i
                if chunk == 0:
                    seen = kept[0][k, p]
                else:
                    seen = jnp.concatenate([kept[0][k, p], kept[1][k, p]], axis=0)
                ratios.append(seen / hold[k, p])
            data = paired(jnp.concatenate(ratios, axis=1), 256)
            section = dot(ayt[chunk, slot], data)
            section = section[:ROWS] + section[ROWS:]
            rows = [section[:, i * QUARTER : (i + 1) * QUARTER] for i in range(many)]
            high, low = halves(jnp.concatenate(rows, axis=0))
            result = dot(jnp.concatenate([high, low], axis=1), wz[slot])
            center = result[:, :128] + result[:, 128:256]
            edge = result[:, 256:384]
            edge = edge + pltpu.roll(edge, 64, 1)
            base = pl.multiple_of(group * (many * SKEW), 8) + k * SLAB * SKEW
            for i in range(many):
                at = base + i * SKEW
                spread[pl.ds(at, ROWS), :] = center[i * ROWS : (i + 1) * ROWS]
                packed = edge[i * ROWS : (i + 1) * ROWS]
                packed = jnp.where(lane < 64, packed[:PACKED], packed[PACKED:])
                spread[pl.ds(at + ROWS, PACKED), :] = packed
            return carry

        lax.fori_loop(0, SLAB // many, planes, 0)

    total = band.shape[1]
    step = 32

    centers = ROWS // step

    def sends(group, edge):
        at = pl.ds(pl.multiple_of(group * step, step), step)
        to = pl.ds(pl.multiple_of((group - edge * centers) * step, step), step)
        targets = outs[0].at[at], outs[1 + 2 * edge].at[to], outs[2 + 2 * edge].at[to]
        return [
            pltpu.make_async_copy(totals[k].at[at], targets[k], out_sems.at[k, group])
            for k in range(3)
        ]

    def some(group, edge):
        at = group * step
        columns = [spread[pl.ds(at + r, n * SLAB, SKEW), :] for r in range(step)]
        result = dot(band[...], paired(jnp.concatenate(columns, axis=1), total))
        result = result[:TALL] + result[TALL:]
        for r in range(step):
            piece = result[:, r * 128 : (r + 1) * 128]
            totals[0][at + r] = piece[:LEFT]
            totals[1][at + r] = piece[LEFT : LEFT + SLAB]
            totals[2][at + r] = piece[LEFT + SLAB :]
        for move in sends(group, edge):
            move.start()
        return edge

    lax.fori_loop(centers, CHUNK // step, lambda group, c: some(group, 1), 1)
    lax.fori_loop(0, centers, lambda group, c: some(group, 0), 0)
    for group in range(CHUNK // step):
        for move in sends(group, int(group >= centers)):
            move.wait()


def adjoint(chunk, spot, band, ayt, wz, forward, recorded, measured, after):
    n = VIEWS
    vmem = pl.BlockSpec(memory_space=pltpu.VMEM)
    hbm = pl.BlockSpec(memory_space=pl.ANY)
    first, last = SPANS[chunk]
    rows = (CUT - first, 128 - CUT)[: chunk + 1]
    sizes = (LEFT, SLAB, RIGHT)
    arrays = [forward]
    for slot in ALL:
        if slot:
            arrays += [measured[piece][slot] for piece in range(chunk + 1)]
        else:
            arrays.append(recorded)
    arrays += after
    return pl.pallas_call(
        lambda *refs: adjoint_kernel(chunk, len(after), *refs),
        out_shape=(shape(CHUNK, LEFT, 128),)
        + tuple(shape(r, k, 128) for r in (ROWS, PACKED) for k in sizes[1:]),
        in_specs=[pl.BlockSpec(memory_space=pltpu.SMEM)] + [vmem] * 3 + [hbm] * len(arrays),
        out_specs=(hbm,) * 5,
        scratch_shapes=[pltpu.VMEM((n, SLAB, last - first, QUARTER), f32)]
        + [pltpu.VMEM((n, SLAB, k, QUARTER), f32) for k in rows]
        + [pltpu.VMEM((n * SLAB * SKEW + 8, 128), f32)]
        + [pltpu.VMEM((CHUNK, k, 128), f32) for k in sizes]
        + [
            pltpu.SemaphoreType.DMA((n, chunk + 2)),
            pltpu.SemaphoreType.DMA((3, CHUNK // 32)),
        ],
        compiler_params=pltpu.CompilerParams(vmem_limit_bytes=VMEM),
        cost_estimate=pl.CostEstimate(flops=FREE, bytes_accessed=FREE, transcendentals=0),
    )(spot, band, ayt, wz, *arrays)


def added(own, up, down):
    half = SLAB // 2
    whole = own[...] + up[...]
    return whole[:, :half], whole[:, half:] + down


def edges_kernel(own, up, down, *refs):
    rights, lefts = refs[-2:]
    near, far = added(own, up, down[ROWS:])
    lane = lax.broadcasted_iota(jnp.int32, (1, SLAB // 2, 128), 2) % 64
    rights[...] = jnp.where(lane < RIGHT, near, pltpu.roll(far, RIGHT, 2))
    lefts[...] = jnp.where(lane < RIGHT + LEFT, near, pltpu.roll(far, LEFT, 2))


def center_kernel(own, up, down, *refs):
    refs[-1][...] = jnp.concatenate(added(own, up, down[:ROWS]), axis=1)


def small(kernel, out_shape, arrays, after, flops):
    vmem = pl.BlockSpec(memory_space=pltpu.VMEM)
    hbm = pl.BlockSpec(memory_space=pl.ANY)
    return pl.pallas_call(
        kernel,
        out_shape=out_shape,
        in_specs=[vmem] * len(arrays) + [hbm] * len(after),
        out_specs=jax.tree.map(lambda _: vmem, out_shape),
        compiler_params=pltpu.CompilerParams(vmem_limit_bytes=VMEM),
        cost_estimate=pl.CostEstimate(flops=flops, bytes_accessed=FREE, transcendentals=0),
    )(*arrays, *after)


def settle_edges(own, up, down, after):
    packed = shape(PACKED, SLAB // 2, 128)
    return small(edges_kernel, (packed, packed), (own, up, down), after, 5 * MICROSECOND)


def settle_center(own, up, down, after):
    return small(center_kernel, shape(ROWS, SLAB, 128), (own, up, down), after, FREE)


def merge_kernel(center, rights, lefts, *refs):
    lane = lax.broadcasted_iota(jnp.int32, (SLAB // 2, 128), 1)
    turns = (((0, 64), (96, 32)), ((80, 16), (64, 0)))
    for piece in (0, 1):
        for r in range(PACKED):
            extra = []
            for group in (0, 1):
                low, high = rights[r], lefts[r]
                if turns[0][group][piece]:
                    low = pltpu.roll(low, turns[0][group][piece], 1)
                if turns[1][group][piece]:
                    high = pltpu.roll(high, turns[1][group][piece], 1)
                high = jnp.where(lane >= QUARTER - LEFT, high, 0.0)
                extra.append(jnp.where(lane < RIGHT, low, high))
            at = piece * PACKED + r
            refs[piece - 2][:, r, :] = center[at] + jnp.concatenate(extra, axis=0)


def merge(center, rights, lefts, after):
    arrays = (center, rights, lefts)
    return small(merge_kernel, (shape(SLAB, PACKED, 128),) * 2, arrays, after, FREE)


def finish_kernel(count, spot, estimate, *refs):
    out = refs[-1]
    first = 0
    for piece in refs[:count]:
        rows = slice(first, first + piece.shape[1])
        out[:, rows, :] = estimate[:, rows, :] * piece[...] / VIEWS
        first = first + piece.shape[1]


def finish(chunk, step, spot, estimate, pieces, before, after):
    n = 16
    place = pl.BlockSpec(
        (n, ROWS, QUARTER), lambda i, s: (i, chunk, lax.rem(s[0] + (VIEWS - step), VIEWS))
    )
    specs = [place] + [
        pl.BlockSpec((n, piece.shape[1], QUARTER), lambda i, s: (i, 0, 0)) for piece in pieces
    ]
    arrays = [spot, estimate, *pieces]
    aliases = {}
    if before is not None:
        specs.append(pl.BlockSpec(memory_space=pl.ANY))
        arrays.append(before)
        aliases = {len(arrays) - 1: 0}
    arrays += after
    specs += [pl.BlockSpec(memory_space=pl.ANY)] * len(after)
    return call(
        lambda *refs: finish_kernel(len(pieces), *refs),
        shape(*estimate.shape),
        (SLAB // n,),
        specs,
        place,
        prefetch=1,
        aliases=aliases,
        flops=FREE,
        moved=FREE,
    )(*arrays)


def along_blk(x, distance):
    size = lax.axis_size("blk")
    route = [(i, i + distance) for i in range(size) if 0 <= i + distance < size]
    return lax.ppermute(x, "blk", route)


def around_view(x, distance):
    return lax.ppermute(x, "view", [(i, (i + distance) % VIEWS) for i in range(VIEWS)])


def along_view(x, distance):
    route = [(i, i + distance) for i in range(VIEWS) if 0 <= i + distance < VIEWS]
    return lax.ppermute(x, "view", route)


def body(estimate, views, psf, offsets):
    q = lax.axis_index("view")
    spot = q[None]
    recorded = views[0]
    middle, last, token, *pieces = window(estimate, spot, recorded)
    upper = along_blk(middle, -1)
    lower = along_blk(last, 1)

    mine = pack(psf[0], offsets[0].astype(f32)[:, None], (token,))
    params = jnp.stack([mine] + [around_view(mine, s) for s in (1, 2, 3)])
    measured = ({s: around_view(piece, s) for s, piece in zip(OTHERS, pieces)}, {})
    starts = jnp.concatenate([params[:, 2, KERN].astype(jnp.int32), spot])
    ax, az, ay, ayt, wz, every = bands(params, ())
    forward, *pieces = forward_of(starts, ax, az, ay, lower, middle, upper, recorded)
    measured[1].update({s: around_view(piece, s) for s, piece in zip(OTHERS, pieces)})

    def spill(parts):
        below, own, above, own_edge, above_edge = parts
        down = along_blk(below, -1)
        return (own_edge, along_blk(above_edge, 1), down), (own, along_blk(above, 1), down)

    def margins(edges):
        rights, lefts = edges
        return along_view(rights, 1), along_view(lefts, -1)

    def gather(piece):
        near, far = piece
        left = around_view(near, 1), around_view(far, 1)
        right = around_view(near, 3), around_view(far, 3)
        opposite = around_view(left[0], 1), around_view(right[1], 3)
        return piece, left, right, opposite

    def adjoint_of(chunk, after):
        return adjoint(chunk, spot, every, ayt, wz, forward, recorded, measured, after)

    parts0 = adjoint_of(0, ())
    spilled0 = spill(parts0)
    margins0 = margins(settle_edges(*spilled0[0], (mark((measured[1][1], measured[1][3]), 16),)))
    center0 = settle_center(*spilled0[1], (measured[1][2],))
    piece0 = merge(center0, *margins0, ())
    gathered0 = gather(piece0)
    parts1 = adjoint_of(1, tuple(piece0))
    spilled1 = spill(parts1)
    margins1 = margins(settle_edges(*spilled1[0], (mark((gathered0[1][0], gathered0[2][1]), 8),)))
    center1 = settle_center(*spilled1[1], ())
    piece1 = merge(center1, *margins1, gathered0[3] + (gathered0[1][1], gathered0[2][0]))
    gathered1 = gather(piece1)
    out = None
    for chunk, gathered in enumerate((gathered0, gathered1)):
        for step, parts in zip((0, 1, 3, 2), gathered):
            after = () if out is not None else (gathered1[1][0], gathered1[2][1])
            out = finish(chunk, step, spot, estimate, parts, out, after)
    return out


def solution(mesh):
    placed = (
        P("blk", None, None),
        P("view", "blk", None, None),
        P("view", None, None),
        P("view", None),
    )
    return jax.shard_map(
        body, mesh=mesh, in_specs=placed, out_specs=P("blk", None, None), check_vma=False
    )
```

```python
import jax
import jax.numpy as jnp
from jax import lax
from jax.experimental import pallas as pl
from jax.experimental.pallas import tpu as pltpu
from jax.sharding import PartitionSpec as P

RADIUS = 16
KERN = 33
LEFT = RADIUS
RIGHT = 2 * RADIUS
QUARTER = 128
WIDE = LEFT + QUARTER + RIGHT
SLAB = 32
TALL = LEFT + SLAB + RIGHT
VIEWS = 4
BACKGROUND = 0.1
ALL = (0, 1, 3, 2)
OTHERS = (1, 3, 2)
ROWS = 64
PACKED = ROWS // 2
CHUNK = ROWS + PACKED
CUT = 80
ODD = WIDE + 1
SKEW = CHUNK + 1
FREE = 1 << 10
MICROSECOND = 1 << 30
SPANS = ((0, 80), (32, 128))
VMEM = 48 * 1024 * 1024

f32 = jnp.float32
bf16 = jnp.bfloat16


def call(kernel, out_shape, grid, in_specs, out_specs, prefetch=0, aliases=None, flops=0, moved=0):
    return pl.pallas_call(
        kernel,
        out_shape=out_shape,
        grid_spec=pltpu.PrefetchScalarGridSpec(
            num_scalar_prefetch=prefetch, grid=grid, in_specs=in_specs, out_specs=out_specs
        ),
        input_output_aliases=aliases or {},
        compiler_params=pltpu.CompilerParams(vmem_limit_bytes=VMEM),
        cost_estimate=pl.CostEstimate(flops=flops, bytes_accessed=moved, transcendentals=0),
    )


def shape(*dims, dtype=f32):
    return jax.ShapeDtypeStruct(dims, dtype)


def halves(x):
    high = x.astype(bf16)
    low = (x - high.astype(f32)).astype(bf16)
    return high, low


def stacked(x, axis, blank=0):
    high, low = halves(x)
    parts = [high, low, high]
    if blank:
        dims = list(x.shape)
        dims[axis] = blank
        parts.append(jnp.zeros(dims, bf16))
    return jnp.concatenate(parts, axis=axis)


def paired(x, total):
    high, low = halves(x)
    parts = [high, low]
    if total > 2 * x.shape[0]:
        parts.append(jnp.zeros((total - 2 * x.shape[0], x.shape[1]), bf16))
    return jnp.concatenate(parts, axis=0)


def dot(a, b):
    return lax.dot_general(a, b, (((1,), (0,)), ((), ())), preferred_element_type=f32)


def dot_nt(a, b):
    return lax.dot_general(a, b, (((1,), (1,)), ((), ())), preferred_element_type=f32)


def lag_taps(params, slot, dim, lag):
    value = jnp.zeros(lag.shape, f32)
    for tap in range(KERN):
        value = jnp.where(lag == tap, params[slot, dim, tap], value)
    return value


def thirds(value, part):
    high = value.astype(bf16).astype(f32)
    return jnp.where(part == 2, value - high, high).astype(bf16)


def split(value):
    high = value.astype(bf16).astype(f32)
    return high, value - high


def grid_of(rows, columns):
    return (
        lax.broadcasted_iota(jnp.int32, (rows, columns), 0),
        lax.broadcasted_iota(jnp.int32, (rows, columns), 1),
    )


def spread_band(params, offset, slots, band):
    total = band.shape[1]
    count = SLAB * len(slots)
    row, lane = grid_of(TALL, total)
    part = lane // count
    spot = lane - part * count
    owner = spot // SLAB
    plane = spot - owner * SLAB
    value = jnp.zeros((TALL, total), f32)
    for place, slot in enumerate(slots):
        lag = plane + offset(slot, 0) - row + 2 * RADIUS
        value = jnp.where(owner == place, lag_taps(params, slot, 0, lag), value)
    high, low = split(value)
    band[:TALL, :] = jnp.where(part < 2, high, 0.0).astype(bf16)
    band[TALL:, :] = jnp.where(part < 1, low, 0.0).astype(bf16)


def bands_kernel(params, *refs):
    ax, az, ay, ayt, wz, every = refs[-6:]

    def offset(slot, dim):
        return params[slot, dim, KERN].astype(jnp.int32)

    row, lane = grid_of(SLAB, 256)
    part = lane // TALL
    spot = lane - part * TALL
    for slot in range(VIEWS):
        lag = row + offset(slot, 0) - spot + 2 * RADIUS
        lag = jnp.where(part < 3, lag, -1)
        ax[slot * SLAB : (slot + 1) * SLAB, :] = thirds(lag_taps(params, slot, 0, lag), part)
    row, lane = grid_of(128, 128)
    part = lane // 32
    tail = lane - part * 32 + 128
    edge = lane % 64
    edge = jnp.where(edge < RIGHT, QUARTER + edge, edge - RIGHT - LEFT)
    for slot in range(VIEWS):
        high, low = split(lag_taps(params, slot, 2, row - lane + 2 * RADIUS))
        az[slot, :, 0:128] = high.astype(bf16)
        az[slot, :, 128:256] = high.astype(bf16)
        az[slot, :, 256:384] = low.astype(bf16)
        lag = jnp.where(part < 3, row - tail + 2 * RADIUS, -1)
        az[slot, :, 384:512] = thirds(lag_taps(params, slot, 2, lag), part)
        high, low = split(lag_taps(params, slot, 1, row + offset(slot, 1) - lane + RADIUS))
        ay[slot, :, 0:128] = high.astype(bf16)
        ay[slot, :, 128:256] = high.astype(bf16)
        ay[slot, :, 256:384] = low.astype(bf16)
        high, low = split(lag_taps(params, slot, 2, row + offset(slot, 2) - lane + RADIUS))
        wz[slot, :128, 0:128] = high.astype(bf16)
        wz[slot, 128:, 0:128] = high.astype(bf16)
        wz[slot, :128, 128:256] = low.astype(bf16)
        wz[slot, 128:, 128:256] = jnp.zeros((128, 128), bf16)
        lag = row + offset(slot, 2) - edge + RADIUS
        lag = jnp.where(lane % 64 < RIGHT + LEFT, lag, -1)
        high, low = split(lag_taps(params, slot, 2, lag))
        wz[slot, :128, 256:384] = jnp.where(lane < 64, high, low).astype(bf16)
        wz[slot, 128:, 256:384] = jnp.where(lane < 64, high, 0.0).astype(bf16)
    row, lane = grid_of(ROWS, 256)
    for chunk, (first, last) in enumerate(SPANS):
        count = last - first
        part = lane // count
        spot = first + lane - part * count
        for slot in range(VIEWS):
            lag = spot + offset(slot, 1) - (row + chunk * ROWS) + RADIUS
            high, low = split(lag_taps(params, slot, 1, lag))
            ayt[chunk, slot, :ROWS, :] = jnp.where(part < 2, high, 0.0).astype(bf16)
            ayt[chunk, slot, ROWS:, :] = jnp.where(part < 1, low, 0.0).astype(bf16)
    spread_band(params, offset, ALL, every)


def bands(params, after):
    whole = pl.BlockSpec(memory_space=pltpu.VMEM)
    shapes = (
        shape(VIEWS * SLAB, 256, dtype=bf16),
        shape(VIEWS, QUARTER, 512, dtype=bf16),
        shape(VIEWS, 128, 384, dtype=bf16),
        shape(2, VIEWS, 2 * ROWS, 256, dtype=bf16),
        shape(VIEWS, 256, 384, dtype=bf16),
        shape(2 * TALL, 256, dtype=bf16),
    )
    return pl.pallas_call(
        bands_kernel,
        out_shape=shapes,
        in_specs=[pl.BlockSpec(memory_space=pltpu.SMEM)]
        + [pl.BlockSpec(memory_space=pl.ANY)] * len(after),
        out_specs=(whole,) * len(shapes),
        compiler_params=pltpu.CompilerParams(vmem_limit_bytes=VMEM),
        cost_estimate=pl.CostEstimate(flops=FREE, bytes_accessed=FREE, transcendentals=0),
    )(params, *after)


def pack_kernel(psf, offsets, *refs):
    out = refs[-1]
    taps = psf[...]
    out[:, :KERN] = taps / jnp.sum(taps, axis=1, keepdims=True)
    out[:, KERN:] = offsets[...]


def pack(psf, offsets, after):
    return small(pack_kernel, shape(3, KERN + 1), (psf, offsets), after, FREE)


def mark_kernel(*refs):
    refs[-1][...] = jnp.zeros(refs[-1].shape, f32)


def mark(after, cost):
    return small(mark_kernel, shape(8, 128), (), after, cost * MICROSECOND)


def cut_moves(first, rows, q, recorded, holds, outs, sems):
    reads, writes = [], []
    for k, step in enumerate(OTHERS):
        quarter = lax.rem(q + step, VIEWS)
        lanes = pl.ds(pl.multiple_of(quarter * QUARTER, QUARTER), QUARTER)
        source = recorded.at[:, pl.ds(first, rows), lanes]
        reads.append(pltpu.make_async_copy(source, holds[k], sems.at[0, k]))
        writes.append(pltpu.make_async_copy(holds[k], outs[k], sems.at[1, k]))
    return reads, writes


def cut_shapes(rows):
    return (shape(SLAB, rows, QUARTER),) * len(OTHERS)


def cut_scratch(rows):
    holds = [pltpu.VMEM((SLAB, rows, QUARTER), f32)] * len(OTHERS)
    return holds + [pltpu.SemaphoreType.DMA((2, len(OTHERS)))]


def cut_steps(step, last, reads, writes):
    @pl.when(step == 0)
    def _():
        for move in reads:
            move.start()

    @pl.when(step == 1)
    def _():
        for move, write in zip(reads, writes):
            move.wait()
            write.start()

    def done():
        @pl.when(step == last)
        def _():
            for write in writes:
                write.wait()

    return done


def window_kernel(spot, left, middle, right, recorded, out, low, token, *refs):
    token[...] = jnp.zeros(token.shape, f32)
    n = len(OTHERS)
    cuts, flat, holds, sems = refs[:n], refs[n], refs[n + 1 : 2 * n + 1], refs[-1]
    q = spot[0]
    moves = cut_moves(0, CUT, q, recorded, holds, cuts, sems)
    done = cut_steps(pl.program_id(0), SLAB // LEFT - 1, *moves)
    planes = middle.shape[0]
    for i in range(planes):
        before = left[i].T[QUARTER - LEFT :, :]
        after = right[i].T[:RIGHT, :]
        at = i * ODD
        flat[at : at + LEFT, :] = jnp.where(q > 0, before, 0.0)
        flat[at + LEFT : at + LEFT + QUARTER, :] = middle[i].T
        flat[at + LEFT + QUARTER : at + WIDE, :] = jnp.where(q < VIEWS - 1, after, 0.0)
    for z in range(WIDE):
        row = flat[pl.ds(z, planes, ODD), :]
        out[z] = row
        low[z] = row
    done()


def window(estimate, spot, recorded):
    hbm = pl.BlockSpec(memory_space=pl.ANY)
    n = LEFT
    block = (n, 128, QUARTER)
    return pl.pallas_call(
        window_kernel,
        out_shape=(shape(WIDE, SLAB, 128), shape(WIDE, LEFT, 128), shape(8, 128))
        + cut_shapes(CUT),
        grid_spec=pltpu.PrefetchScalarGridSpec(
            num_scalar_prefetch=1,
            grid=(SLAB // n,),
            in_specs=[
                pl.BlockSpec(block, lambda i, s: (i, 0, jnp.maximum(s[0] - 1, 0))),
                pl.BlockSpec(block, lambda i, s: (i, 0, s[0])),
                pl.BlockSpec(block, lambda i, s: (i, 0, jnp.minimum(s[0] + 1, VIEWS - 1))),
                hbm,
            ],
            out_specs=(
                pl.BlockSpec((WIDE, n, 128), lambda i, s: (0, i, 0)),
                pl.BlockSpec((WIDE, n, 128), lambda i, s: (0, 0, 0)),
                pl.BlockSpec((8, 128), lambda i, s: (0, 0)),
            )
            + (hbm,) * len(OTHERS),
            scratch_shapes=[pltpu.VMEM(((n + 1) * ODD + 7, 128), f32)] + cut_scratch(CUT),
        ),
        compiler_params=pltpu.CompilerParams(vmem_limit_bytes=62 * 1024 * 1024),
        cost_estimate=pl.CostEstimate(flops=FREE, bytes_accessed=FREE, transcendentals=0),
    )(spot, estimate, estimate, estimate, recorded)


def forward_kernel(starts, ax, az, ay, lower, middle, upper, recorded, out, *refs):
    n = len(OTHERS)
    cuts, refs = refs[:n], refs[n:]
    blurred, planes_of, load_sems = refs[0], refs[1:4], refs[4]
    holds, sems = refs[5:-1], refs[-1]
    slot = pl.program_id(0)
    moves = cut_moves(CUT, 128 - CUT, starts[VIEWS], recorded, holds, cuts, sems)
    done = cut_steps(slot, VIEWS - 1, *moves)
    step = 16

    def loads(group):
        at = pl.ds(pl.multiple_of(group * step, step), step)
        return [
            pltpu.make_async_copy(ref.at[at], planes_of[k].at[at], load_sems.at[k, group])
            for k, ref in enumerate((lower, middle, upper))
        ]

    @pl.when(slot == 0)
    def _():
        for group in range(WIDE // step):
            for move in loads(group):
                move.start()

        def some(group, carry):
            for move in loads(group):
                move.wait()
            at = group * step
            columns = [
                jnp.concatenate([ref[at + z] for ref in planes_of], axis=0) for z in range(step)
            ]
            data = stacked(jnp.concatenate(columns, axis=1), 0, 256 - 3 * TALL)
            result = dot(ax[...], data)
            for z in range(step):
                blurred[pl.ds(at + z, VIEWS * SLAB, ODD), :] = result[:, z * 128 : z * 128 + 128]
            return carry

        lax.fori_loop(0, WIDE // step, some, 0)

    start = starts[slot]
    span = QUARTER + 2 * RADIUS
    many = SLAB

    def planes(group, carry):
        first = slot * SLAB + group * many
        data = jnp.concatenate(
            [blurred[pl.ds((first + i) * ODD + start, span), :] for i in range(many)], axis=1
        )
        high, low = halves(data)
        blank = jnp.zeros((32, many * 128), bf16)
        data = [high[:128], low[:128], high[:128], high[128:], low[128:], high[128:], blank]
        section = dot(az[0], jnp.concatenate(data, axis=0))
        section = jnp.concatenate([section[:, i * 128 : i * 128 + 128] for i in range(many)], axis=0)
        result = dot_nt(ay[0], stacked(section, 1)) + BACKGROUND
        for i in range(many):
            out[group * many + i] = result[:, i * QUARTER : (i + 1) * QUARTER]
        return carry

    lax.fori_loop(0, SLAB // many, planes, 0)
    done()


def forward_of(starts, ax, az, ay, lower, middle, upper, recorded):
    hbm = pl.BlockSpec(memory_space=pl.ANY)
    rows = 128 - CUT

    def once(x):
        return pl.BlockSpec(x.shape, lambda v, s: (0,) * x.ndim, pipeline_mode=pl.Buffered(1))

    return pl.pallas_call(
        forward_kernel,
        out_shape=(shape(VIEWS * SLAB, 128, QUARTER),) + cut_shapes(rows),
        grid_spec=pltpu.PrefetchScalarGridSpec(
            num_scalar_prefetch=1,
            grid=(VIEWS,),
            in_specs=[
                once(ax),
                pl.BlockSpec((1,) + az.shape[1:], lambda v, s: (v, 0, 0)),
                pl.BlockSpec((1,) + ay.shape[1:], lambda v, s: (v, 0, 0)),
                hbm,
                hbm,
                hbm,
                hbm,
            ],
            out_specs=(pl.BlockSpec((SLAB, 128, QUARTER), lambda v, s: (v, 0, 0)),)
            + (hbm,) * len(OTHERS),
            scratch_shapes=[pltpu.VMEM(((VIEWS * SLAB + 1) * ODD + 7, 128), f32)]
            + [pltpu.VMEM(x.shape, f32) for x in (lower, middle, upper)]
            + [pltpu.SemaphoreType.DMA((3, WIDE // 16))]
            + cut_scratch(rows),
        ),
        compiler_params=pltpu.CompilerParams(vmem_limit_bytes=VMEM),
        cost_estimate=pl.CostEstimate(flops=FREE, bytes_accessed=FREE, transcendentals=0),
    )(starts, ax, az, ay, lower, middle, upper, recorded)


def adjoint_kernel(chunk, extra, *refs):
    n = VIEWS
    pieces = chunk + 1
    first, last = SPANS[chunk]
    bounds = ((first, CUT), (CUT, 128))[:pieces]
    spot, band, ayt, wz, forward = refs[:5]
    refs = list(refs[5:])
    measured = []
    for slot in ALL:
        if slot == 0:
            lanes = pl.ds(pl.multiple_of(spot[0] * QUARTER, QUARTER), QUARTER)
            whole = refs.pop(0)
            measured.append([whole.at[:, pl.ds(a, b - a), lanes] for a, b in bounds])
        else:
            measured.append([refs.pop(0).at[:, pl.ds(first, CUT - first), :]])
            if chunk:
                measured[-1].append(refs.pop(0))
    refs = refs[extra:]
    outs, refs = refs[:5], refs[5:]
    hold, kept, spread = refs[0], refs[1 : 1 + pieces], refs[1 + pieces]
    totals = refs[2 + pieces : 5 + pieces]
    sems, out_sems = refs[-2:]
    copies = []
    for k, slot in enumerate(ALL):
        source = forward.at[pl.ds(slot * SLAB, SLAB), pl.ds(first, last - first), :]
        moves = [pltpu.make_async_copy(source, hold.at[k], sems.at[k, 0])]
        for piece in range(pieces):
            target = kept[piece].at[k]
            moves.append(pltpu.make_async_copy(measured[k][piece], target, sems.at[k, 1 + piece]))
        for move in moves:
            move.start()
        copies.append(moves)

    many = SLAB
    lane = lax.broadcasted_iota(jnp.int32, (PACKED, 128), 1)
    for k, slot in enumerate(ALL):
        for move in copies[k]:
            move.wait()

        def planes(group, carry, k=k, slot=slot):
            ratios = []
            for i in range(many):
                p = group * many + i
                if chunk == 0:
                    seen = kept[0][k, p]
                else:
                    seen = jnp.concatenate([kept[0][k, p], kept[1][k, p]], axis=0)
                ratios.append(seen / hold[k, p])
            data = paired(jnp.concatenate(ratios, axis=1), 256)
            section = dot(ayt[chunk, slot], data)
            section = section[:ROWS] + section[ROWS:]
            rows = [section[:, i * QUARTER : (i + 1) * QUARTER] for i in range(many)]
            high, low = halves(jnp.concatenate(rows, axis=0))
            result = dot(jnp.concatenate([high, low], axis=1), wz[slot])
            center = result[:, :128] + result[:, 128:256]
            edge = result[:, 256:384]
            edge = edge + pltpu.roll(edge, 64, 1)
            base = pl.multiple_of(group * (many * SKEW), 8) + k * SLAB * SKEW
            for i in range(many):
                at = base + i * SKEW
                spread[pl.ds(at, ROWS), :] = center[i * ROWS : (i + 1) * ROWS]
                packed = edge[i * ROWS : (i + 1) * ROWS]
                packed = jnp.where(lane < 64, packed[:PACKED], packed[PACKED:])
                spread[pl.ds(at + ROWS, PACKED), :] = packed
            return carry

        lax.fori_loop(0, SLAB // many, planes, 0)

    total = band.shape[1]
    step = 32

    centers = ROWS // step

    def sends(group, edge):
        at = pl.ds(pl.multiple_of(group * step, step), step)
        to = pl.ds(pl.multiple_of((group - edge * centers) * step, step), step)
        targets = outs[0].at[at], outs[1 + 2 * edge].at[to], outs[2 + 2 * edge].at[to]
        return [
            pltpu.make_async_copy(totals[k].at[at], targets[k], out_sems.at[k, group])
            for k in range(3)
        ]

    def some(group, edge):
        at = group * step
        columns = [spread[pl.ds(at + r, n * SLAB, SKEW), :] for r in range(step)]
        result = dot(band[...], paired(jnp.concatenate(columns, axis=1), total))
        result = result[:TALL] + result[TALL:]
        for r in range(step):
            piece = result[:, r * 128 : (r + 1) * 128]
            totals[0][at + r] = piece[:LEFT]
            totals[1][at + r] = piece[LEFT : LEFT + SLAB]
            totals[2][at + r] = piece[LEFT + SLAB :]
        for move in sends(group, edge):
            move.start()
        return edge

    lax.fori_loop(centers, CHUNK // step, lambda group, c: some(group, 1), 1)
    lax.fori_loop(0, centers, lambda group, c: some(group, 0), 0)
    for group in range(CHUNK // step):
        for move in sends(group, int(group >= centers)):
            move.wait()


def adjoint(chunk, spot, band, ayt, wz, forward, recorded, measured, after):
    n = VIEWS
    vmem = pl.BlockSpec(memory_space=pltpu.VMEM)
    hbm = pl.BlockSpec(memory_space=pl.ANY)
    first, last = SPANS[chunk]
    rows = (CUT - first, 128 - CUT)[: chunk + 1]
    sizes = (LEFT, SLAB, RIGHT)
    arrays = [forward]
    for slot in ALL:
        if slot:
            arrays += [measured[piece][slot] for piece in range(chunk + 1)]
        else:
            arrays.append(recorded)
    arrays += after
    return pl.pallas_call(
        lambda *refs: adjoint_kernel(chunk, len(after), *refs),
        out_shape=(shape(CHUNK, LEFT, 128),)
        + tuple(shape(r, k, 128) for r in (ROWS, PACKED) for k in sizes[1:]),
        in_specs=[pl.BlockSpec(memory_space=pltpu.SMEM)] + [vmem] * 3 + [hbm] * len(arrays),
        out_specs=(hbm,) * 5,
        scratch_shapes=[pltpu.VMEM((n, SLAB, last - first, QUARTER), f32)]
        + [pltpu.VMEM((n, SLAB, k, QUARTER), f32) for k in rows]
        + [pltpu.VMEM(((n * SLAB + 1) * SKEW + 7, 128), f32)]
        + [pltpu.VMEM((CHUNK, k, 128), f32) for k in sizes]
        + [
            pltpu.SemaphoreType.DMA((n, chunk + 2)),
            pltpu.SemaphoreType.DMA((3, CHUNK // 32)),
        ],
        compiler_params=pltpu.CompilerParams(vmem_limit_bytes=VMEM),
        cost_estimate=pl.CostEstimate(flops=FREE, bytes_accessed=FREE, transcendentals=0),
    )(spot, band, ayt, wz, *arrays)


def added(own, up, down):
    half = SLAB // 2
    whole = own[...] + up[...]
    return whole[:, :half], whole[:, half:] + down


def edges_kernel(own, up, down, *refs):
    rights, lefts = refs[-2:]
    near, far = added(own, up, down[ROWS:])
    lane = lax.broadcasted_iota(jnp.int32, (1, SLAB // 2, 128), 2) % 64
    rights[...] = jnp.where(lane < RIGHT, near, pltpu.roll(far, RIGHT, 2))
    lefts[...] = jnp.where(lane < RIGHT + LEFT, near, pltpu.roll(far, LEFT, 2))


def center_kernel(own, up, down, *refs):
    refs[-1][...] = jnp.concatenate(added(own, up, down[:ROWS]), axis=1)


def small(kernel, out_shape, arrays, after, flops):
    vmem = pl.BlockSpec(memory_space=pltpu.VMEM)
    hbm = pl.BlockSpec(memory_space=pl.ANY)
    return pl.pallas_call(
        kernel,
        out_shape=out_shape,
        in_specs=[vmem] * len(arrays) + [hbm] * len(after),
        out_specs=jax.tree.map(lambda _: vmem, out_shape),
        compiler_params=pltpu.CompilerParams(vmem_limit_bytes=VMEM),
        cost_estimate=pl.CostEstimate(flops=flops, bytes_accessed=FREE, transcendentals=0),
    )(*arrays, *after)


def settle_edges(own, up, down, after):
    packed = shape(PACKED, SLAB // 2, 128)
    return small(edges_kernel, (packed, packed), (own, up, down), after, 5 * MICROSECOND)


def settle_center(own, up, down, after):
    return small(center_kernel, shape(ROWS, SLAB, 128), (own, up, down), after, FREE)


def merge_kernel(center, rights, lefts, *refs):
    lane = lax.broadcasted_iota(jnp.int32, (SLAB // 2, 128), 1)
    turns = (((0, 64), (96, 32)), ((80, 16), (64, 0)))
    for piece in (0, 1):
        for r in range(PACKED):
            extra = []
            for group in (0, 1):
                low, high = rights[r], lefts[r]
                if turns[0][group][piece]:
                    low = pltpu.roll(low, turns[0][group][piece], 1)
                if turns[1][group][piece]:
                    high = pltpu.roll(high, turns[1][group][piece], 1)
                high = jnp.where(lane >= QUARTER - LEFT, high, 0.0)
                extra.append(jnp.where(lane < RIGHT, low, high))
            at = piece * PACKED + r
            refs[piece - 2][:, r, :] = center[at] + jnp.concatenate(extra, axis=0)


def merge(center, rights, lefts, after):
    arrays = (center, rights, lefts)
    return small(merge_kernel, (shape(SLAB, PACKED, 128),) * 2, arrays, after, FREE)


def finish_kernel(count, spot, estimate, *refs):
    out = refs[-1]
    first = 0
    for piece in refs[:count]:
        rows = slice(first, first + piece.shape[1])
        out[:, rows, :] = estimate[:, rows, :] * piece[...] / VIEWS
        first = first + piece.shape[1]


def finish(chunk, step, spot, estimate, pieces, before, after):
    n = 16
    place = pl.BlockSpec(
        (n, ROWS, QUARTER), lambda i, s: (i, chunk, lax.rem(s[0] + (VIEWS - step), VIEWS))
    )
    specs = [place] + [
        pl.BlockSpec((n, piece.shape[1], QUARTER), lambda i, s: (i, 0, 0)) for piece in pieces
    ]
    arrays = [spot, estimate, *pieces]
    aliases = {}
    if before is not None:
        specs.append(pl.BlockSpec(memory_space=pl.ANY))
        arrays.append(before)
        aliases = {len(arrays) - 1: 0}
    arrays += after
    specs += [pl.BlockSpec(memory_space=pl.ANY)] * len(after)
    return call(
        lambda *refs: finish_kernel(len(pieces), *refs),
        shape(*estimate.shape),
        (SLAB // n,),
        specs,
        place,
        prefetch=1,
        aliases=aliases,
        flops=FREE,
        moved=FREE,
    )(*arrays)


def along_blk(x, distance):
    size = lax.axis_size("blk")
    route = [(i, i + distance) for i in range(size) if 0 <= i + distance < size]
    return lax.ppermute(x, "blk", route)


def around_view(x, distance):
    return lax.ppermute(x, "view", [(i, (i + distance) % VIEWS) for i in range(VIEWS)])


def along_view(x, distance):
    route = [(i, i + distance) for i in range(VIEWS) if 0 <= i + distance < VIEWS]
    return lax.ppermute(x, "view", route)


def body(estimate, views, psf, offsets):
    q = lax.axis_index("view")
    spot = q[None]
    recorded = views[0]
    middle, last, token, *pieces = window(estimate, spot, recorded)
    upper = along_blk(middle, -1)
    lower = along_blk(last, 1)

    mine = pack(psf[0], offsets[0].astype(f32)[:, None], (token,))
    params = jnp.stack([mine] + [around_view(mine, s) for s in (1, 2, 3)])
    measured = ({s: around_view(piece, s) for s, piece in zip(OTHERS, pieces)}, {})
    starts = jnp.concatenate([params[:, 2, KERN].astype(jnp.int32), spot])
    ax, az, ay, ayt, wz, every = bands(params, ())
    forward, *pieces = forward_of(starts, ax, az, ay, lower, middle, upper, recorded)
    measured[1].update({s: around_view(piece, s) for s, piece in zip(OTHERS, pieces)})

    def spill(parts):
        below, own, above, own_edge, above_edge = parts
        down = along_blk(below, -1)
        return (own_edge, along_blk(above_edge, 1), down), (own, along_blk(above, 1), down)

    def margins(edges):
        rights, lefts = edges
        return along_view(rights, 1), along_view(lefts, -1)

    def gather(piece):
        near, far = piece
        left = around_view(near, 1), around_view(far, 1)
        right = around_view(near, 3), around_view(far, 3)
        opposite = around_view(left[0], 1), around_view(right[1], 3)
        return piece, left, right, opposite

    def adjoint_of(chunk, after):
        return adjoint(chunk, spot, every, ayt, wz, forward, recorded, measured, after)

    parts0 = adjoint_of(0, ())
    spilled0 = spill(parts0)
    margins0 = margins(settle_edges(*spilled0[0], (mark((measured[1][1], measured[1][3]), 16),)))
    center0 = settle_center(*spilled0[1], (measured[1][2],))
    piece0 = merge(center0, *margins0, ())
    gathered0 = gather(piece0)
    parts1 = adjoint_of(1, tuple(piece0))
    spilled1 = spill(parts1)
    margins1 = margins(settle_edges(*spilled1[0], (mark((gathered0[1][0], gathered0[2][1]), 8),)))
    center1 = settle_center(*spilled1[1], ())
    piece1 = merge(center1, *margins1, gathered0[3] + (gathered0[1][1], gathered0[2][0]))
    gathered1 = gather(piece1)
    out = None
    for chunk, gathered in enumerate((gathered0, gathered1)):
        for step, parts in zip((0, 1, 3, 2), gathered):
            after = () if out is not None else (gathered1[1][0], gathered1[2][1])
            out = finish(chunk, step, spot, estimate, parts, out, after)
    return out


def solution(mesh):
    placed = (
        P("blk", None, None),
        P("view", "blk", None, None),
        P("view", None, None),
        P("view", None),
    )
    return jax.shard_map(
        body, mesh=mesh, in_specs=placed, out_specs=P("blk", None, None), check_vma=False
    )
```
